32 devices in a mesh: space: 4 (over y, core), terms: 8 (over z, x).
Axes of the slice: x: 2, y: 2, z: 4, core: 2. Of those that a mesh axis runs over, the one named last changes fastest.
Arguments:
- forcing: float32 [144, 3, 8, 32, 128], P('terms', None, 'space'), may hold values from -6 to 6
- stencil: float32 [27, 3, 3], replicated, may hold values from -0.12 to 3, as said below
- fields: float32 [5, 8, 32, 128], P(None, 'space'), may hold values from -3 to 3
- coupling: float32 [126, 5], replicated, may hold values from 0.25 to 1
- slot_term: int32 [144], replicated, may hold values from -1 to 125, as said below
Outputs:
- solution: float32 [144, 3, 8, 32, 128], P('terms', None, 'space')
The draws below stay inside these ranges and needn't reach their ends.
Inputs may be any that keep to these rules, and one draw needn't show every extreme that they name: `slot_term`: device k of terms holds the slots k * 18 to (k + 1) * 18 - 1; of these, the first 1 hold level-0 terms or -1, the next 1 level 1, then 2 level 2, 5 level 3 and 9 level 4. Every term stands in exactly one slot. The central diagonal entries stencil[13, a, a] lie in 2 to 3; every other entry lies in -0.12 to 0.05.
All inputs are finite; a program needn't handle non-finite values.
Results may differ from the reference program's by a relative error of at most 0.00014.
Values sent between devices are 32-bit elements; how exact they have to be, the bound alone decides.
No kernel may reach another device: no remote copies, remote signals or barrier semaphores. Data moves between devices by JAX's collectives and lax.ppermute only.
A program may use at most 128 MiB of HBM per device.

```python
import math
import jax
import jax.numpy as jnp
import numpy as np
from jax import lax

DIMS = 5
DEGREE = 4
TERMS = 126
NY = 32
NZ = 128
NX = 8
SLOTS_L0 = 1
SLOTS_L1 = 1
SLOTS_L2 = 2
SLOTS_L3 = 5
SLOTS_L4 = 9
SLOT_DEV = 18
SLOTS = 144


def draw_stencil(key, part):
    subkeys = jax.random.split(key, 3)
    offsets = jnp.arange(27)[:, None, None]
    rows_index = jnp.arange(3)[None, :, None]
    cols_index = jnp.arange(3)[None, None, :]
    same_comp = rows_index == cols_index
    central = offsets == 13
    along = jax.random.uniform(subkeys[0], (27, 3, 3), minval=-0.12, maxval=-0.02)
    across = jax.random.uniform(subkeys[1], (27, 3, 3), minval=-0.05, maxval=0.05)
    pivot_draw = jax.random.uniform(subkeys[2], (27, 3, 3), minval=2.0, maxval=3.0)
    table = jnp.where(central & same_comp, pivot_draw, jnp.where(same_comp, along, across))
    return table.astype(jnp.float32)


def draw_slot_term(key, part):
    groups_count = SLOTS // SLOT_DEV
    level_caps = [SLOTS_L0, SLOTS_L1, SLOTS_L2, SLOTS_L3, SLOTS_L4]
    pieces = []
    first_term = 0
    for level_now in range(DEGREE + 1):
        level_count = math.comb(level_now + DIMS - 1, DIMS - 1)
        extent = groups_count * level_caps[level_now]
        shuffled = jax.random.permutation(jax.random.fold_in(key, level_now + 11), extent)
        values = jnp.where(shuffled < level_count, shuffled + first_term, -1).astype(jnp.int32)
        pieces.append(values.reshape(groups_count, level_caps[level_now]))
        first_term += level_count
    return jnp.concatenate(pieces, axis=1).reshape(-1)


def level_of(own_key, shape, cuts, low, largest):
    factor_of = 1.0
    for position, shards_of in cuts:
        heights = jax.random.uniform(jax.random.fold_in(jax.random.fold_in(own_key, 6), position), (shards_of,), jnp.float32, low / len(cuts), largest / len(cuts))
        factor_of = factor_of * jnp.repeat(jnp.exp(heights), shape[position] // shards_of).reshape((-1,) + (1,) * (len(shape) - 1 - position))
    return factor_of


def gaussian(stream_key, shape, scale, bound, shards=(), held_as=jnp.bfloat16):
    values = scale * jax.random.normal(stream_key, shape, jnp.float32)
    if shards:
        values = values * level_of(stream_key, shape, shards, -0.22, 0.18)
    return jnp.clip(values, -bound, bound).astype(held_as)


def setup_inputs(seed: int = 0) -> dict:
    keys = jax.random.split(jax.random.key(seed), 6)
    return {
        "forcing": gaussian(keys[0], (SLOTS, 3, NX, NY, NZ), 1.0, 6.0, ((0, 8), (2, 4)), jnp.float32),
        "stencil": draw_stencil(jax.random.fold_in(keys[5], 71), 0),
        "fields": gaussian(keys[2], (DIMS, NX, NY, NZ), 0.5, 3.0, ((1, 4),), jnp.float32),
        "coupling": jnp.clip(jnp.exp(jax.random.uniform(keys[3], (TERMS, DIMS), jnp.float32, math.log(0.25), math.log(1.0))), 0.25, 1.0),
        "slot_term": draw_slot_term(jax.random.fold_in(keys[5], 71), 0),
    }


def compositions(total, pieces_left):
    if pieces_left == 1:
        return [[total]]
    result = []
    for leading in range(total, -1, -1):
        for remainder in compositions(total - leading, pieces_left - 1):
            result.append([leading] + remainder)
    return result


def chaos_parents(dimensions, top_degree):
    indices = []
    for level_now in range(top_degree + 1):
        indices.extend(compositions(level_now, dimensions))
    lookup = {}
    for number, vector in enumerate(indices):
        lookup[tuple(vector)] = number
    parents = np.full((len(indices), dimensions), -1, dtype=np.int32)
    for number, vector in enumerate(indices):
        for dimension in range(dimensions):
            if vector[dimension] > 0:
                lowered = list(vector)
                lowered[dimension] -= 1
                parents[number, dimension] = lookup[tuple(lowered)]
    return parents


def shifted(array, offset, axis_dim):
    if offset == 0:
        return array
    length = array.shape[axis_dim]
    zeros_edge = jnp.zeros_like(lax.slice_in_dim(array, 0, 1, axis=axis_dim))
    if offset > 0:
        return jnp.concatenate([lax.slice_in_dim(array, 1, length, axis=axis_dim), zeros_edge], axis=axis_dim)
    return jnp.concatenate([zeros_edge, lax.slice_in_dim(array, 0, length - 1, axis=axis_dim)], axis=axis_dim)


def apply_stencil(extended, stencil):
    inner_x = extended.shape[2] - 2
    summed = jnp.zeros(extended.shape[:2] + (inner_x,) + extended.shape[3:], jnp.float32)
    for step_y in range(3):
        for step_z in range(3):
            moved_yz = shifted(shifted(extended, step_y - 1, 3), step_z - 1, 4)
            for step_x in range(3):
                window = lax.slice_in_dim(moved_yz, step_x, step_x + inner_x, axis=2)
                block_coef = stencil[9 * step_x + 3 * step_y + step_z]
                summed = summed + jnp.einsum('ab,sbxyz->saxyz', block_coef, window, precision=lax.Precision.HIGHEST)
    return summed


def pad_first(field):
    return jnp.pad(field, ((0, 0), (0, 0), (1, 1), (0, 0), (0, 0)))


def reference(forcing, stencil, fields, coupling, slot_term):
    parents = chaos_parents(DIMS, DEGREE)
    safe_slots = jnp.where(slot_term >= 0, slot_term, TERMS).astype(jnp.int32)
    slot_of = jnp.zeros((TERMS + 1,), jnp.int32).at[safe_slots].set(jnp.arange(SLOTS, dtype=jnp.int32))
    ordered = forcing[slot_of[:TERMS]]
    pivots = jnp.diagonal(stencil[13])[None, :, None, None, None]
    solutions = []
    images = []
    offset = 0
    for level_now in range(DEGREE + 1):
        level_count = math.comb(level_now + DIMS - 1, DIMS - 1)
        level_load = ordered[offset:offset + level_count]
        if level_now > 0:
            known_images = jnp.concatenate(images, axis=0)
            for dimension in range(DIMS):
                linked = parents[offset:offset + level_count, dimension]
                present = linked >= 0
                picked = known_images[np.where(present, linked, 0)]
                weight = coupling[offset:offset + level_count, dimension] * jnp.asarray(present, jnp.float32)
                level_load = level_load - weight[:, None, None, None, None] * fields[dimension][None, None] * picked
        first_pass = level_load / pivots
        settled = first_pass + (level_load - apply_stencil(pad_first(first_pass), stencil)) / pivots
        solutions.append(settled)
        if level_now < DEGREE:
            images.append(apply_stencil(pad_first(settled), stencil))
        offset += level_count
    ordered_solution = jnp.concatenate(solutions + [jnp.zeros_like(solutions[0][:1])], axis=0)
    return ordered_solution[safe_slots]
```

```python
import functools
import math

import jax
import jax.numpy as jnp
import numpy as np
from jax import lax
from jax.experimental import pallas as pl
from jax.experimental.pallas import tpu as pltpu
from jax.sharding import PartitionSpec as P

DIMS = 5
DEGREE = 4
F32 = jnp.float32
BF16 = jnp.bfloat16
VMEM = pl.BlockSpec(memory_space=pltpu.VMEM)
SMEM = pl.BlockSpec(memory_space=pltpu.SMEM)
PARAMS = pltpu.CompilerParams(vmem_limit_bytes=56 * 2**20)


def compositions(total, pieces_left):
    if pieces_left == 1:
        return [[total]]
    result = []
    for leading in range(total, -1, -1):
        for remainder in compositions(total - leading, pieces_left - 1):
            result.append([leading] + remainder)
    return result


def chaos_links():
    indices = []
    for level in range(DEGREE + 1):
        indices.extend(compositions(level, DIMS))
    lookup = {tuple(vector): number for number, vector in enumerate(indices)}
    dims = np.zeros((len(indices), DEGREE), np.int32)
    parents = np.full((len(indices), DEGREE), -1, np.int32)
    for number, vector in enumerate(indices):
        place = 0
        for dim in range(DIMS):
            if vector[dim] > 0:
                lowered = list(vector)
                lowered[dim] -= 1
                dims[number, place] = dim
                parents[number, place] = lookup[tuple(lowered)]
                place += 1
    return dims, parents


LINK_DIMS, LINK_PARENTS = chaos_links()
COUNTS = [math.comb(level + DIMS - 1, DIMS - 1) for level in range(DEGREE + 1)]
FIRSTS = [sum(COUNTS[:level]) for level in range(DEGREE + 1)]


def stencil_matrix(stencil, rows):
    taps = stencil.reshape(3, 3, 3, 3, 3)
    place = np.arange(rows)
    total = 0.0
    for step in range(3):
        band = jnp.asarray((place[None, :] == place[:, None] + step - 1).astype(np.float32))
        part = jnp.transpose(taps[:, step], (1, 2, 0, 3))
        total = total + part[:, :, None, :, :, None] * band[None, None, :, None, None, :]
    return total.reshape(9 * rows, 9 * rows)


def split_matrix(matrix_ref, packed_ref):
    size = matrix_ref.shape[1]
    high = matrix_ref[...].astype(BF16)
    packed_ref[:, :size] = high
    packed_ref[:, size : 2 * size] = high
    packed_ref[:, 2 * size :] = (matrix_ref[...] - high.astype(F32)).astype(BF16)


def put_split(value, high_ref, low_ref, place):
    high = value.astype(BF16)
    high_ref[place] = high
    low_ref[place] = (value - high.astype(F32)).astype(BF16)


def apply_pair(high_ref, low_ref, packed_ref, place):
    def window(ref):
        return [jnp.concatenate([ref[place + k], ref[place + k + 1]], axis=1) for k in range(3)]

    high = window(high_ref)
    operand = jnp.concatenate(high + window(low_ref) + high, axis=0)
    product = jnp.dot(packed_ref[...], operand, preferred_element_type=F32)
    lanes = high_ref.shape[2]
    size = high_ref.shape[1]
    lane = lax.broadcasted_iota(jnp.int32, (size, lanes), 1)
    results = []
    for half in range(2):
        block = product[:, half * lanes : (half + 1) * lanes]
        before = pltpu.roll(block[:size], 1, 1)
        after = pltpu.roll(block[2 * size :], lanes - 1, 1)
        results.append(block[size : 2 * size] + jnp.where(lane > 0, before, 0.0) + jnp.where(lane < lanes - 1, after, 0.0))
    return results


def inverse_pivots(inverse_ref, rows, lanes):
    return jnp.concatenate([jnp.full((rows, lanes), inverse_ref[a], F32) for a in range(3)], axis=0)


def sweep_kernel(terms, edge_ref, inverse_ref, matrix_ref, load_ref, even_ref, odd_ref, settled_ref, image_ref, packed, high, low, high2, low2):
    rows, lanes = load_ref.shape[3:]
    size = 3 * rows
    split_matrix(matrix_ref, packed)
    inverse = inverse_pivots(inverse_ref, rows, lanes)
    is_even = edge_ref[0] > 0.5
    has_lower = edge_ref[1]
    has_upper = edge_ref[2]

    def layer(ref, term, x):
        return ref[term, :, x].reshape(size, lanes)

    def one(term, carry):
        def load(x):
            if 2 <= x < 4:
                return layer(load_ref, term, x - 2)
            if x < 2:
                return jnp.where(is_even, layer(odd_ref, term, x), layer(even_ref, term, x))
            return jnp.where(is_even, layer(even_ref, term, x - 4), layer(odd_ref, term, x - 4))

        for x in range(6):
            put_split(load(x) * inverse, high, low, x)
        for pair in range(2):
            applied = apply_pair(high, low, packed, 2 * pair)
            for half in range(2):
                x = 2 * pair + half + 1
                load_x = load(x)
                settled = load_x * inverse + (load_x - applied[half]) * inverse
                if x == 1:
                    settled = settled * has_lower
                if x == 4:
                    settled = settled * has_upper
                if 2 <= x < 4:
                    settled_ref[term, :, x - 2] = settled.reshape(3, rows, lanes)
                put_split(settled, high2, low2, x - 1)
        applied = apply_pair(high2, low2, packed, 0)
        for half in range(2):
            image_ref[term, :, half] = applied[half].reshape(3, rows, lanes)
        return carry

    lax.fori_loop(0, terms, one, 0)


def last_kernel(terms, edge_ref, inverse_ref, matrix_ref, load_ref, even_ref, odd_ref, settled_ref, packed, high, low):
    rows, lanes = load_ref.shape[3:]
    size = 3 * rows
    split_matrix(matrix_ref, packed)
    inverse = inverse_pivots(inverse_ref, rows, lanes)
    is_even = edge_ref[0] > 0.5

    def one(term, carry):
        even = even_ref[term, :, 0].reshape(size, lanes)
        odd = odd_ref[term, :, 0].reshape(size, lanes)
        put_split(jnp.where(is_even, odd, even) * inverse, high, low, 0)
        put_split(jnp.where(is_even, even, odd) * inverse, high, low, 3)
        for x in range(2):
            put_split(load_ref[term, :, x].reshape(size, lanes) * inverse, high, low, x + 1)
        applied = apply_pair(high, low, packed, 0)
        for x in range(2):
            load = load_ref[term, :, x].reshape(size, lanes)
            settled = load * inverse + (load - applied[x]) * inverse
            settled_ref[term, :, x] = settled.reshape(3, rows, lanes)
        return carry

    lax.fori_loop(0, terms, one, 0)


def load_kernel(terms, cap, blocks, slot_ref, dim_ref, block_ref, row_ref, weight_ref, forcing_ref, fields_ref, *refs):
    image_refs = refs[:blocks]
    load_ref, images = refs[blocks:]
    for block in range(blocks):
        images[block * cap : (block + 1) * cap] = image_refs[block][...]

    def one(term, carry):
        total = forcing_ref[slot_ref[term]] * weight_ref[term, DEGREE]
        for link in range(DEGREE):
            place = block_ref[term, link] * cap + row_ref[term, link]
            field = fields_ref[dim_ref[term, link]] * weight_ref[term, link]
            total = total - field[None] * images[place]
        load_ref[term] = total
        return carry

    lax.fori_loop(0, terms, one, 0)


def run_sweep(load, even, odd, edge, inverse, matrix):
    terms, _, _, rows, lanes = load.shape
    size = 3 * rows
    out = jax.ShapeDtypeStruct(load.shape, F32)
    return pl.pallas_call(
        functools.partial(sweep_kernel, terms),
        out_shape=[out, out],
        in_specs=[SMEM, SMEM] + [VMEM] * 4,
        out_specs=[VMEM, VMEM],
        scratch_shapes=[pltpu.VMEM((3 * size, 9 * size), BF16)]
        + [pltpu.VMEM((6, size, lanes), BF16)] * 2
        + [pltpu.VMEM((4, size, lanes), BF16)] * 2,
        compiler_params=PARAMS,
        cost_estimate=pl.CostEstimate(flops=2 * 3 * terms * 27 * size * size * 256, bytes_accessed=20 * load.size, transcendentals=0),
        name="sweep",
    )(edge, inverse, matrix, load, even, odd)


def run_last(load, even, odd, edge, inverse, matrix):
    terms, _, _, rows, lanes = load.shape
    size = 3 * rows
    return pl.pallas_call(
        functools.partial(last_kernel, terms),
        out_shape=jax.ShapeDtypeStruct(load.shape, F32),
        in_specs=[SMEM, SMEM] + [VMEM] * 4,
        out_specs=VMEM,
        scratch_shapes=[pltpu.VMEM((3 * size, 9 * size), BF16)] + [pltpu.VMEM((4, size, lanes), BF16)] * 2,
        compiler_params=PARAMS,
        cost_estimate=pl.CostEstimate(flops=2 * terms * 27 * size * size * 256, bytes_accessed=12 * load.size, transcendentals=0),
        name="last_sweep",
    )(edge, inverse, matrix, load, even, odd)


def run_load(terms, slots, links, weights, forcing, fields, images):
    cap = images[0].shape[0]
    blocks = len(images)
    return pl.pallas_call(
        functools.partial(load_kernel, terms, cap, blocks),
        out_shape=jax.ShapeDtypeStruct((terms,) + forcing.shape[1:], F32),
        in_specs=[SMEM] * 5 + [VMEM] * (2 + blocks),
        out_specs=VMEM,
        scratch_shapes=[pltpu.VMEM((cap * blocks,) + forcing.shape[1:], F32)],
        compiler_params=PARAMS,
        cost_estimate=pl.CostEstimate(flops=12 * terms * forcing[0].size, bytes_accessed=4 * cap * blocks * forcing[0].size, transcendentals=0),
        name="loads",
    )(slots, *links, weights, forcing, fields, *images)


def beside(array, axis, stride):
    count = lax.axis_size(axis)
    even = [(i, i ^ 1) for i in range(count)]
    odd = [(i, ((i + 1) ^ 1) - 1) for i in range(1, count - 1)]
    return lax.ppermute(array[0], axis, even), lax.ppermute(array[1], axis, odd)


def gather_blocks(block, index):
    count = lax.axis_size("terms")
    if count != 8:
        whole = lax.all_gather(block, "terms", axis=0, tiled=False)
        return [whole[i] for i in range(count)], jnp.arange(count, dtype=jnp.int32)

    def columns(pairs):
        return [(2 * i + x, 2 * j + x) for i, j in pairs for x in range(2)]

    ends = columns([(0, 1), (1, 0), (2, 3), (3, 2)])
    middle = columns([(1, 2), (2, 1)])
    outward = columns([(1, 0), (2, 3)])
    across = [(i, i ^ 1) for i in range(8)]

    def send(array, pairs):
        return lax.ppermute(array, "terms", pairs)

    near = send(block, ends)
    middle_one = send(block, middle)
    second = middle_one + send(middle_one, outward)
    middle_two = send(near, middle)
    third = middle_two + send(middle_two, outward)
    own = [block, near, second, third]
    order = np.array([[0, 1, 2, 3], [1, 0, 2, 3], [3, 2, 0, 1], [3, 2, 1, 0]], np.int32)
    place = jnp.asarray(order)[index // 2]
    places = [place[source // 2] + 4 * ((index ^ source) & 1) for source in range(8)]
    return own + [send(array, across) for array in own], jnp.stack(places).astype(jnp.int32)


def on_device(forcing, stencil, fields, coupling, slot_term):
    groups = lax.axis_size("terms")
    slabs = lax.axis_size("space")
    slot_dev = forcing.shape[0]
    group = lax.axis_index("terms")
    slab = lax.axis_index("space")
    caps = [(count + groups - 1) // groups for count in COUNTS]
    starts = [sum(caps[:level]) for level in range(DEGREE + 1)]
    rows = forcing.shape[3]

    matrix = stencil_matrix(stencil, rows)
    inverse = 1.0 / jnp.diagonal(stencil[13])
    is_even = slab % 2 == 0
    edge = jnp.stack([is_even, slab > 0, slab < slabs - 1]).astype(F32)
    table = slot_term.reshape(groups, slot_dev)
    mine = lax.dynamic_index_in_dim(table, group, 0, keepdims=False)
    slot_of = jnp.sum(
        jnp.where(slot_term[None, :] == jnp.arange(126, dtype=jnp.int32)[:, None], jnp.arange(slot_term.shape[0], dtype=jnp.int32)[None, :], 0),
        axis=1,
    ).astype(jnp.int32)
    dims = jnp.asarray(LINK_DIMS)
    parents = jnp.asarray(np.maximum(LINK_PARENTS, 0))
    weights = jnp.where(jnp.asarray(LINK_PARENTS >= 0), jnp.take_along_axis(coupling, dims, axis=1), 0.0)
    weights = jnp.concatenate([weights, jnp.ones((126, 1), F32)], axis=1)

    def level_slots(level):
        return forcing[starts[level] : starts[level] + caps[level]]

    def slot_tables(level):
        ids = mine[starts[level] : starts[level] + caps[level]]
        filled = ids >= 0
        safe = jnp.maximum(ids, 0)
        weight = weights[safe] * filled.astype(F32)[:, None]
        return safe, weight, filled

    filled0 = (mine[:1] >= 0).astype(F32)[:, None, None, None, None]
    load0 = level_slots(0) * filled0
    strides = [1 << bit for bit in range(groups.bit_length() - 1)]
    strides = strides[1:] + strides[:1]
    for stride in strides:
        load0 = load0 + lax.ppermute(load0, "terms", [(i, i ^ stride) for i in range(groups)])
    gathered, offsets = level_slots(1), [0]
    for stride in strides:
        gathered = jnp.concatenate([gathered, lax.ppermute(gathered, "terms", [(i, i ^ stride) for i in range(groups)])], axis=0)
        offsets = offsets + [offset ^ stride for offset in offsets]
    offset_place = np.zeros((groups,), np.int32)
    offset_place[offsets] = np.arange(groups)

    settled0, image0 = run_sweep(load0, *beside((load0, load0), "space", 1), edge, inverse, matrix)
    source1 = slot_of[FIRSTS[1] : FIRSTS[1] + DIMS] // slot_dev
    slots1 = jnp.asarray(offset_place)[source1 ^ group]
    zeros = jnp.zeros((DIMS, DEGREE), jnp.int32)
    load1 = run_load(DIMS, slots1, (dims[1:6], zeros, zeros), weights[1:6], gathered, fields, [image0])
    settled1, image1 = run_sweep(load1, *beside((load1, load1), "space", 1), edge, inverse, matrix)

    settled = [settled0 * filled0]
    safe1, _, filled1 = slot_tables(1)
    own1 = lax.dynamic_slice_in_dim(settled1, jnp.clip(safe1[0] - 1, 0, DIMS - 1), 1, axis=0)
    settled.append(jnp.where(filled1[0], own1, 0.0))

    images, places, held = [image1], None, None
    for level in range(2, DEGREE + 1):
        safe, weight, _ = slot_tables(level)
        parent = parents[safe]
        if level == 2:
            block = jnp.zeros_like(parent)
            row = jnp.maximum(parent - FIRSTS[1], 0)
        else:
            slot = slot_of[parent]
            block = places[slot // slot_dev]
            row = jnp.clip(slot % slot_dev - starts[level - 1], 0, caps[level - 1] - 1)
        load = run_load(caps[level], jnp.arange(caps[level], dtype=jnp.int32), (dims[safe], block, row), weight, level_slots(level), fields, images)
        if level < DEGREE:
            result, image = run_sweep(load, *beside((load, load), "space", 1), edge, inverse, matrix)
            images, places = gather_blocks(image, group)
        else:
            head, tail = load[:, :, :1], load[:, :, 1:]
            pieces = (jnp.where(is_even, tail, head), jnp.where(is_even, head, tail))
            result = run_last(load, *beside(pieces, "space", 1), edge, inverse, matrix)
        settled.append(result)
    return jnp.concatenate(settled, axis=0)


def solution(mesh):
    return jax.shard_map(
        on_device,
        mesh=mesh,
        in_specs=(
            P("terms", None, "space", None, None),
            P(),
            P(None, "space", None, None),
            P(),
            P(),
        ),
        out_specs=P("terms", None, "space", None, None),
        check_vma=False,
    )
```

```python
import functools
import math

import jax
import jax.numpy as jnp
import numpy as np
from jax import lax
from jax.experimental import pallas as pl
from jax.experimental.pallas import tpu as pltpu
from jax.sharding import PartitionSpec as P

DIMS = 5
DEGREE = 4
F32 = jnp.float32
BF16 = jnp.bfloat16
ANY = pl.BlockSpec(memory_space=pl.ANY)
VMEM = pl.BlockSpec(memory_space=pltpu.VMEM)
SMEM = pl.BlockSpec(memory_space=pltpu.SMEM)
PARAMS = pltpu.CompilerParams(vmem_limit_bytes=20 * 2**20)


def compositions(total, pieces_left):
    if pieces_left == 1:
        return [[total]]
    result = []
    for leading in range(total, -1, -1):
        for remainder in compositions(total - leading, pieces_left - 1):
            result.append([leading] + remainder)
    return result


def chaos_links():
    indices = []
    for level in range(DEGREE + 1):
        indices.extend(compositions(level, DIMS))
    lookup = {tuple(vector): number for number, vector in enumerate(indices)}
    dims = np.zeros((len(indices), DEGREE), np.int32)
    parents = np.full((len(indices), DEGREE), -1, np.int32)
    for number, vector in enumerate(indices):
        place = 0
        for dim in range(DIMS):
            if vector[dim] > 0:
                lowered = list(vector)
                lowered[dim] -= 1
                dims[number, place] = dim
                parents[number, place] = lookup[tuple(lowered)]
                place += 1
    return dims, parents


LINK_DIMS, LINK_PARENTS = chaos_links()
LINKS = np.concatenate([LINK_PARENTS, LINK_DIMS], axis=1).T.astype(np.int32)
COUNTS = [math.comb(level + DIMS - 1, DIMS - 1) for level in range(DEGREE + 1)]
FIRSTS = [sum(COUNTS[:level]) for level in range(DEGREE + 1)]


def prologue_kernel(slot_ref, forcing_ref, out_ref):
    slot_dev = forcing_ref.shape[0]
    pltpu.sync_copy(forcing_ref.at[pl.ds(0, 2)], out_ref)
    filled = slot_ref[lax.axis_index("terms") * slot_dev] >= 0
    out_ref[0] = jnp.where(filled, out_ref[0], 0.0)


def matrix_kernel(stencil_ref, packed_ref):
    size = packed_ref.shape[1] // 3
    rows = size // 9
    lane = lax.broadcasted_iota(jnp.int32, (rows, size), 1)
    shift = lane % rows - lax.broadcasted_iota(jnp.int32, (rows, size), 0) + 1
    column = lane // rows
    for oz in range(3):
        for a in range(3):
            block = jnp.zeros((rows, size), F32)
            for oy in range(3):
                taps = jnp.zeros((rows, size), F32)
                for ox in range(3):
                    for b in range(3):
                        taps = jnp.where(column == 3 * ox + b, stencil_ref[a, b, 9 * ox + 3 * oy + oz], taps)
                block = jnp.where(shift == oy, taps, block)
            high = block.astype(BF16)
            place = pl.ds((3 * oz + a) * rows, rows)
            packed_ref[place, :size] = high
            packed_ref[place, size : 2 * size] = high
            packed_ref[place, 2 * size :] = (block - high.astype(F32)).astype(BF16)


def put_split(value, high_ref, low_ref, place):
    high = value.astype(BF16)
    high_ref[place] = high
    low_ref[place] = (value - high.astype(F32)).astype(BF16)


def apply_pair(high_ref, low_ref, packed_ref, place):
    def window(ref):
        return [jnp.concatenate([ref[place + k], ref[place + k + 1]], axis=1) for k in range(3)]

    high = window(high_ref)
    operand = jnp.concatenate(high + window(low_ref) + high, axis=0)
    product = jnp.dot(packed_ref[...], operand, preferred_element_type=F32)
    lanes = high_ref.shape[2]
    size = high_ref.shape[1]
    lane = lax.broadcasted_iota(jnp.int32, (size, lanes), 1)
    results = []
    for half in range(2):
        block = product[:, half * lanes : (half + 1) * lanes]
        before = pltpu.roll(block[:size], 1, 1)
        after = pltpu.roll(block[2 * size :], lanes - 1, 1)
        results.append(block[size : 2 * size] + jnp.where(lane > 0, before, 0.0) + jnp.where(lane < lanes - 1, after, 0.0))
    return results


def inverse_pivots(stencil_ref, rows, lanes):
    return jnp.concatenate([1.0 / jnp.full((rows, lanes), stencil_ref[a, a, 13], F32) for a in range(3)], axis=0)


def sweep_terms(terms, stencil_ref, packed, load_ref, even_ref, odd_ref, settled_ref, images, high, low, high2, low2):
    rows, lanes = load_ref.shape[3:]
    size = 3 * rows
    inverse = inverse_pivots(stencil_ref, rows, lanes)
    slab = lax.axis_index("space")
    is_even = slab % 2 == 0
    has_lower = slab > 0
    has_upper = slab < lax.axis_size("space") - 1

    def layer(ref, term, x):
        return ref[term, :, x].reshape(size, lanes)

    for term in range(terms):

        def load(x):
            if 2 <= x < 4:
                return layer(load_ref, term, x - 2)
            if x < 2:
                return jnp.where(is_even, layer(odd_ref, term, x), layer(even_ref, term, x))
            return jnp.where(is_even, layer(even_ref, term, x - 4), layer(odd_ref, term, x - 4))

        for x in range(6):
            put_split(load(x) * inverse, high.at[term], low.at[term], x)
        for pair in range(2):
            applied = apply_pair(high.at[term], low.at[term], packed, 2 * pair)
            for half in range(2):
                x = 2 * pair + half + 1
                load_x = load(x)
                settled = load_x * inverse + (load_x - applied[half]) * inverse
                if x == 1:
                    settled = jnp.where(has_lower, settled, 0.0)
                if x == 4:
                    settled = jnp.where(has_upper, settled, 0.0)
                if 2 <= x < 4:
                    settled_ref[term, :, x - 2] = settled.reshape(3, rows, lanes)
                put_split(settled, high2.at[term], low2.at[term], x - 1)
        applied = apply_pair(high2.at[term], low2.at[term], packed, 0)
        for half in range(2):
            images[term][:, half] = applied[half].reshape(3, rows, lanes)


def sweep_kernel(parts, stencil_ref, packed, load_ref, even_ref, odd_ref, settled_ref, *refs):
    images = [ref.at[i] for ref, part in zip(refs, parts, strict=False) for i in range(part)]
    sweep_terms(sum(parts), stencil_ref, packed, load_ref, even_ref, odd_ref, settled_ref, images, *refs[len(parts) :])


def child_load(links, group, slot_dev, start, slot, slot_ref, coupling_ref, links_ref, forcing, fields, image_of):
    child = slot_ref[group * slot_dev + start + slot]
    filled = child >= 0
    child = jnp.maximum(child, 0)
    total = forcing[slot]
    for link in range(links):
        parent = links_ref[link, child]
        dim = links_ref[DEGREE + link, child]
        weight = jnp.where(parent >= 0, coupling_ref[dim, child], 0.0)
        total = total - (fields[dim] * weight)[None] * image_of(jnp.maximum(parent, 0))
    return jnp.where(filled, total, 0.0)


def sweep_one_kernel(cap, start, slot_ref, coupling_ref, links_ref, stencil_ref, packed, load_ref, even_ref, odd_ref, fields_ref, forcing_ref, settled_ref, next_ref, image_ref, forcing, *scratch):
    slot_dev = forcing_ref.shape[0]
    pltpu.sync_copy(forcing_ref.at[pl.ds(start, cap)], forcing)
    sweep_terms(DIMS, stencil_ref, packed, load_ref, even_ref, odd_ref, settled_ref, [image_ref.at[i] for i in range(DIMS)], *scratch)
    group = lax.axis_index("terms")
    for slot in range(cap):
        next_ref[slot] = child_load(
            2, group, slot_dev, start, slot, slot_ref, coupling_ref, links_ref, forcing, fields_ref, lambda parent: image_ref[jnp.clip(parent - 1, 0, DIMS - 1)]
        )


def first_load_kernel(groups, slot_dev, slot_ref, coupling_ref, order_ref, fields_ref, image_ref, *refs):
    load_ref, gathered_ref, place = refs[-3:]
    for pair in range(groups // 2):
        gathered_ref[2 * pair : 2 * pair + 2] = refs[pair][...]
    group = lax.axis_index("terms")
    for source in range(groups):
        term = slot_ref[source * slot_dev + 1]

        @pl.when(term >= 0)
        def _():
            place[jnp.maximum(term, 0)] = order_ref[group, source]

    for dim in range(DIMS):
        load_ref[dim] = gathered_ref[place[dim + 1]] - (fields_ref[dim] * coupling_ref[dim, dim + 1])[None] * image_ref[0]


def load_kernel(level, cap, start, parts, old_start, blocks, slot_ref, coupling_ref, links_ref, order_ref, fields_ref, forcing_ref, *refs):
    old_cap = sum(parts)
    image_refs = refs[: blocks * len(parts)]
    load_ref = refs[len(image_refs)]
    pieces = refs[len(image_refs) + 1 : -3]
    images, forcing, place = refs[-3:]
    slot_dev = forcing_ref.shape[0]
    group = lax.axis_index("terms")
    pltpu.sync_copy(forcing_ref.at[pl.ds(start, cap)], forcing)
    for source in range(blocks):
        for slot in range(old_cap):
            term = slot_ref[source * slot_dev + old_start + slot]

            @pl.when(term >= 0)
            def _():
                place[jnp.maximum(term, 0)] = order_ref[group, source] * old_cap + slot

    for block in range(blocks):
        offset = block * old_cap
        for number, part in enumerate(parts):
            images[offset : offset + part] = image_refs[number * blocks + block][...]
            offset += part
    is_even = lax.axis_index("space") % 2 == 0
    for slot in range(cap):

        def image_of(parent):
            return images[jnp.clip(place[parent], 0, blocks * old_cap - 1)]

        load = child_load(level, group, slot_dev, start, slot, slot_ref, coupling_ref, links_ref, forcing, fields_ref, image_of)
        load_ref[slot] = load
        if pieces:
            pieces[0][slot] = jnp.where(is_even, load[:, 1], load[:, 0])
            pieces[1][slot] = jnp.where(is_even, load[:, 0], load[:, 1])


def last_kernel(starts, caps, slot_ref, stencil_ref, packed, load_ref, even_ref, odd_ref, zero_ref, one_ref, two_ref, three_ref, out_ref, high, low):
    rows, lanes = load_ref.shape[3:]
    size = 3 * rows
    slot_dev = out_ref.shape[0]
    first = lax.axis_index("terms") * slot_dev
    out_ref[0] = jnp.where(slot_ref[first] >= 0, zero_ref[0], 0.0)
    own = slot_ref[first + 1]
    out_ref[1] = jnp.where(own >= 0, one_ref[jnp.clip(own - 1, 0, DIMS - 1)], 0.0)
    out_ref[starts[2] : starts[2] + caps[2]] = two_ref[...]
    out_ref[starts[3] : starts[3] + caps[3]] = three_ref[...]
    inverse = inverse_pivots(stencil_ref, rows, lanes)
    is_even = lax.axis_index("space") % 2 == 0
    for term in range(caps[4]):
        even = even_ref[term].reshape(size, lanes)
        odd = odd_ref[term].reshape(size, lanes)
        put_split(jnp.where(is_even, odd, even) * inverse, high.at[term], low.at[term], 0)
        put_split(jnp.where(is_even, even, odd) * inverse, high.at[term], low.at[term], 3)
        for x in range(2):
            put_split(load_ref[term, :, x].reshape(size, lanes) * inverse, high.at[term], low.at[term], x + 1)
        applied = apply_pair(high.at[term], low.at[term], packed, 0)
        for x in range(2):
            load = load_ref[term, :, x].reshape(size, lanes)
            settled = load * inverse + (load - applied[x]) * inverse
            out_ref[starts[4] + term, :, x] = settled.reshape(3, rows, lanes)


def split_scratch(terms, layers, size, lanes):
    return [pltpu.VMEM((terms, layers, size, lanes), BF16)] * 2


def cost(flops, operands):
    return pl.CostEstimate(flops=flops, bytes_accessed=sum(4 * math.prod(o.shape) for o in operands), transcendentals=0)


def call(kernel, out_shape, specs, scratch, operands, name, flops=0):
    single = not isinstance(out_shape, list)
    return pl.pallas_call(
        kernel,
        out_shape=out_shape,
        in_specs=specs,
        out_specs=VMEM if single else [VMEM] * len(out_shape),
        scratch_shapes=scratch,
        compiler_params=PARAMS,
        cost_estimate=cost(flops, operands),
        name=name,
    )(*operands)


def beside(array, axis):
    count = lax.axis_size(axis)
    even = [(i, i ^ 1) for i in range(count)]
    odd = [(i, ((i + 1) ^ 1) - 1) for i in range(1, count - 1)]
    return lax.ppermute(array[0], axis, even), lax.ppermute(array[1], axis, odd)


def gather_blocks(block):
    count = lax.axis_size("terms")
    if count != 8:
        whole = lax.all_gather(block, "terms", axis=0, tiled=False)
        return [whole[i] for i in range(count)], np.tile(np.arange(count, dtype=np.int32), (count, 1))

    def columns(pairs):
        return [(2 * i + x, 2 * j + x) for i, j in pairs for x in range(2)]

    ends = columns([(0, 1), (1, 0), (2, 3), (3, 2)])
    middle = columns([(1, 2), (2, 1)])
    outward = columns([(1, 0), (2, 3)])
    across = [(i, i ^ 1) for i in range(8)]

    def send(array, pairs):
        return lax.ppermute(array, "terms", pairs)

    near, middle_one, across_own = lax.optimization_barrier((send(block, ends), send(block, middle), send(block, across)))
    second = middle_one + send(middle_one, outward)
    middle_two, second, across_near = lax.optimization_barrier((send(near, middle), second, send(near, across)))
    third = middle_two + send(middle_two, outward)
    third, across_second = lax.optimization_barrier((third, send(second, across)))
    column = np.array([[0, 1, 2, 3], [1, 0, 2, 3], [3, 2, 0, 1], [3, 2, 1, 0]], np.int32)
    order = [[column[i // 2, j // 2] + 4 * ((i ^ j) & 1) for j in range(8)] for i in range(8)]
    return [block, near, second, third, across_own, across_near, across_second, send(third, across)], np.array(order, np.int32)


def on_device(forcing, stencil, fields, coupling, slot_term):
    groups = lax.axis_size("terms")
    slot_dev = forcing.shape[0]
    group = lax.axis_index("terms")
    caps = [(count + groups - 1) // groups for count in COUNTS]
    starts = [sum(caps[:level]) for level in range(DEGREE + 1)]
    rows, lanes = forcing.shape[3:]
    size = 3 * rows
    field = forcing.shape[1:]

    def array(*shape):
        return jax.ShapeDtypeStruct(shape, F32)

    taps = jnp.transpose(stencil, (1, 2, 0))
    weights = coupling.T
    links = jnp.asarray(LINKS)
    first = call(prologue_kernel, array(2, *field), [SMEM, ANY], [], [slot_term, forcing], "prologue")
    packed = call(matrix_kernel, jax.ShapeDtypeStruct((3 * size, 9 * size), BF16), [SMEM], [], [taps], "matrix")

    def swap(operand, stride):
        return lax.ppermute(operand, "terms", [(i, i ^ stride) for i in range(groups)])

    other = swap(first, 1)
    load = first[:1] + other[:1]
    pair = jnp.concatenate([first[1:], other[1:]], axis=0)
    gathered, offsets = [pair], [0, 1]
    for offset in range(2, groups, 2):
        gathered.append(swap(pair, offset))
        offsets += [offset, offset ^ 1]
    stride = 2
    while stride < groups:
        load = load + swap(load, stride)
        stride *= 2
    order = np.zeros((groups, groups), np.int32)
    for device in range(groups):
        for place, offset in enumerate(offsets):
            order[device, device ^ offset] = place

    def dots(count):
        return count * 2 * 27 * size * size * 256

    def sweep(level_load, parts):
        terms = sum(parts)
        operands = [taps, packed, level_load, *beside((level_load, level_load), "space")]
        scratch = split_scratch(terms, 6, size, lanes) + split_scratch(terms, 4, size, lanes)
        shapes = [array(terms, *field)] + [array(part, *field) for part in parts]
        return call(functools.partial(sweep_kernel, parts), shapes, [SMEM] + [VMEM] * 4, scratch, operands, "sweep", dots(3 * terms))

    settled0, image0 = sweep(load, (1,))
    load = call(
        functools.partial(first_load_kernel, groups, slot_dev),
        array(DIMS, *field),
        [SMEM] * 3 + [VMEM] * (2 + len(gathered)),
        [pltpu.VMEM((groups, *field), F32), pltpu.SMEM((128,), jnp.int32)],
        [slot_term, weights, jnp.asarray(order), fields, image0, *gathered],
        "first_loads",
    )
    settled1, load = call(
        functools.partial(sweep_one_kernel, caps[2], starts[2]),
        [array(DIMS, *field), array(caps[2], *field)],
        [SMEM] * 4 + [VMEM] * 5 + [ANY],
        [pltpu.VMEM((DIMS, *field), F32), pltpu.VMEM((caps[2], *field), F32)] + split_scratch(DIMS, 6, size, lanes) + split_scratch(DIMS, 4, size, lanes),
        [slot_term, weights, links, taps, packed, load, *beside((load, load), "space"), fields, forcing],
        "sweep_one",
        dots(3 * DIMS),
    )
    settled = [settled0, settled1]
    for level in (3, 4):
        old = caps[level - 1]
        parts = (old,)
        result, *images = sweep(load, parts)
        settled.append(result)
        blocks = []
        for image in images:
            gathered, order = gather_blocks(image)
            blocks += gathered
        shapes = [array(caps[level], *field)]
        if level == DEGREE:
            shapes += [array(caps[level], 3, rows, lanes)] * 2
        load, *pieces = call(
            functools.partial(load_kernel, level, caps[level], starts[level], parts, starts[level - 1], groups),
            shapes,
            [SMEM] * 4 + [VMEM, ANY] + [VMEM] * len(blocks),
            [pltpu.VMEM((old * groups, *field), F32), pltpu.VMEM((caps[level], *field), F32), pltpu.SMEM((128,), jnp.int32)],
            [slot_term, weights, links, jnp.asarray(order), fields, forcing, *blocks],
            "loads",
        )
    return call(
        functools.partial(last_kernel, starts, caps),
        array(*forcing.shape),
        [SMEM] * 2 + [VMEM] * 8,
        split_scratch(caps[4], 4, size, lanes),
        [slot_term, taps, packed, load, *beside(pieces, "space"), *settled],
        "last_sweep",
        dots(caps[4]),
    )


def solution(mesh):
    return jax.shard_map(
        on_device,
        mesh=mesh,
        in_specs=(
            P("terms", None, "space", None, None),
            P(),
            P(None, "space", None, None),
            P(),
            P(),
        ),
        out_specs=P("terms", None, "space", None, None),
        check_vma=False,
    )
```

```python
import functools
import math

import jax
import jax.numpy as jnp
import numpy as np
from jax import lax
from jax.experimental import pallas as pl
from jax.experimental.pallas import tpu as pltpu
from jax.sharding import PartitionSpec as P

DIMS = 5
DEGREE = 4
UNROLL = 5
F32 = jnp.float32
BF16 = jnp.bfloat16
ANY = pl.BlockSpec(memory_space=pl.ANY)
VMEM = pl.BlockSpec(memory_space=pltpu.VMEM)
HBM = pl.BlockSpec(memory_space=pltpu.HBM)
SMEM = pl.BlockSpec(memory_space=pltpu.SMEM)


def compositions(total, pieces_left):
    if pieces_left == 1:
        return [[total]]
    result = []
    for leading in range(total, -1, -1):
        for remainder in compositions(total - leading, pieces_left - 1):
            result.append([leading] + remainder)
    return result


def chaos_links():
    indices = []
    for level in range(DEGREE + 1):
        indices.extend(compositions(level, DIMS))
    lookup = {tuple(vector): number for number, vector in enumerate(indices)}
    dims = np.zeros((len(indices), DEGREE), np.int32)
    parents = np.full((len(indices), DEGREE), -1, np.int32)
    for number, vector in enumerate(indices):
        place = 0
        for dim in range(DIMS):
            if vector[dim] > 0:
                lowered = list(vector)
                lowered[dim] -= 1
                dims[number, place] = dim
                parents[number, place] = lookup[tuple(lowered)]
                place += 1
    return dims, parents


LINK_DIMS, LINK_PARENTS = chaos_links()
COUNTS = [math.comb(level + DIMS - 1, DIMS - 1) for level in range(DEGREE + 1)]
FIRSTS = [sum(COUNTS[:level]) for level in range(DEGREE + 1)]


def matrix_kernel(stencil_ref, packed_ref):
    fill_matrix(0, stencil_ref, packed_ref)


def fill_matrix(shift, stencil_ref, packed_ref):
    size = packed_ref.shape[1] // 3
    rows = size // 9
    out_rows = packed_ref.shape[0] // 9
    lane = lax.broadcasted_iota(jnp.int32, (out_rows, size), 1)
    step = lane % rows - lax.broadcasted_iota(jnp.int32, (out_rows, size), 0) + (1 - shift)
    column = lane // rows
    for oz in range(3):
        for a in range(3):
            block = jnp.zeros((out_rows, size), F32)
            for oy in range(3):
                taps = jnp.zeros((out_rows, size), F32)
                for ox in range(3):
                    for b in range(3):
                        taps = jnp.where(column == 3 * ox + b, stencil_ref[a, b, 9 * ox + 3 * oy + oz], taps)
                block = jnp.where(step == oy, taps, block)
            high = block.astype(BF16)
            place = pl.ds((3 * oz + a) * out_rows, out_rows)
            packed_ref[place, :size] = high
            packed_ref[place, size : 2 * size] = high
            packed_ref[place, 2 * size :] = (block - high.astype(F32)).astype(BF16)


def put_split(value, high_ref, low_ref, place):
    high = value.astype(BF16)
    high_ref[place] = high
    low_ref[place] = (value - high.astype(F32)).astype(BF16)


def apply_pair(high_ref, low_ref, packed_ref, place):
    def window(ref):
        return [jnp.concatenate([ref[place + k], ref[place + k + 1]], axis=1) for k in range(3)]

    high = window(high_ref)
    operand = jnp.concatenate(high + window(low_ref) + high, axis=0)
    product = jnp.dot(packed_ref[...], operand, preferred_element_type=F32)
    lanes = high_ref.shape[2]
    size = packed_ref.shape[0] // 3
    lane = lax.broadcasted_iota(jnp.int32, (size, lanes), 1)
    results = []
    for half in range(2):
        block = product[:, half * lanes : (half + 1) * lanes]
        before = pltpu.roll(block[:size], 1, 1)
        after = pltpu.roll(block[2 * size :], lanes - 1, 1)
        results.append(block[size : 2 * size] + jnp.where(lane > 0, before, 0.0) + jnp.where(lane < lanes - 1, after, 0.0))
    return results


def start_copies(sources, targets, semaphores):
    copies = [pltpu.make_async_copy(source, target, semaphores.at[i]) for i, (source, target) in enumerate(zip(sources, targets, strict=True))]
    for copy in copies:
        copy.start()
    return copies


def eight(rows):
    return (rows + 7) // 8 * 8


def inverse_pivots(stencil_ref, rows, lanes):
    return jnp.concatenate([1.0 / jnp.full((rows, lanes), stencil_ref[a, a, 13], F32) for a in range(3)], axis=0)


def edge_flags():
    slab = lax.axis_index("space")
    return slab % 2 == 0, slab > 0, slab < lax.axis_size("space") - 1


def window(start, width, rows):
    first = max(start, 0)
    last = min(start + width, rows)
    return first, first - start, last - first


def fields_window(own, halo, fields_ref, out):
    group = lax.axis_index("terms")
    rows, lanes = fields_ref.shape[2:]
    width = own + 2 * halo
    for case in range(lax.axis_size("terms")):

        @pl.when(group == case)
        def _():
            first, place, length = window(own * case - halo, width, rows)
            for dim in range(DIMS):
                for plane in range(6):
                    base = plane * width
                    if place:
                        out[dim, base : base + place] = jnp.zeros((place, lanes), F32)
                    out[dim, base + place : base + place + length] = fields_ref[dim, plane % 2, first : first + length]
                    if place + length < width:
                        out[dim, base + place + length : base + width] = jnp.zeros((width - place - length, lanes), F32)


def places(place, start, cap, stride, offset, groups, slot_dev, slot_ref):
    for source in range(groups):
        for slot in range(cap):
            term = slot_ref[source * slot_dev + start + slot]
            place[jnp.where(term >= 0, term, 127)] = source * stride + offset + slot


def own_kernel(own, first, layout, stencil_ref, packed, forcing_ref, even_ref, odd_ref, settled_ref, out_ref, image, high, low, high2, low2):
    rows, lanes = forcing_ref.shape[3:]
    size = 3 * rows
    groups = out_ref.shape[0]
    inverse = inverse_pivots(stencil_ref, rows, lanes)
    is_even, has_lower, has_upper = edge_flags()

    def load(number, x):
        slot = first + number
        if 2 <= x < 4:
            return forcing_ref[slot, :, x - 2].reshape(size, lanes)
        even = even_ref[slot, :, x % 2].reshape(size, lanes)
        odd = odd_ref[slot, :, x % 2].reshape(size, lanes)
        return jnp.where(is_even, odd, even) if x < 2 else jnp.where(is_even, even, odd)

    for number in range(len(layout)):
        for x in range(6):
            put_split(load(number, x) * inverse, high.at[number], low.at[number], x)
    for number in range(len(layout)):
        for pair in range(2):
            applied = apply_pair(high.at[number], low.at[number], packed, 2 * pair)
            for half in range(2):
                x = 2 * pair + half + 1
                load_x = load(number, x)
                value = load_x * inverse + (load_x - applied[half]) * inverse
                if x == 1:
                    value = jnp.where(has_lower, value, 0.0)
                if x == 4:
                    value = jnp.where(has_upper, value, 0.0)
                if 2 <= x < 4:
                    settled_ref[number, :, x - 2] = value.reshape(3, rows, lanes)
                put_split(value, high2.at[number], low2.at[number], x - 1)
    for number, (halo, row) in enumerate(layout):
        applied = apply_pair(high2.at[number], low2.at[number], packed, 0)
        for x in range(2):
            image[number, x] = applied[x]
        width = own + 2 * halo
        for group in range(groups):
            begin, place, length = window(own * group - halo, width, rows)
            for plane in range(6):
                target = row + plane * width
                start = plane // 2 * rows + begin
                if place:
                    out_ref[group, target : target + place] = jnp.zeros((place, lanes), F32)
                out_ref[group, target + place : target + place + length] = image[number, plane % 2, start : start + length]
                if place + length < width:
                    out_ref[group, target + place + length : target + width] = jnp.zeros((width - place - length, lanes), F32)


def own_last_kernel(first, stencil_ref, packed, forcing_ref, even_ref, odd_ref, settled_ref, high, low):
    rows, lanes = forcing_ref.shape[3:]
    size = 3 * rows
    inverse = inverse_pivots(stencil_ref, rows, lanes)
    is_even = edge_flags()[0]
    for number in range(settled_ref.shape[0]):
        even = even_ref[number].reshape(size, lanes)
        odd = odd_ref[number].reshape(size, lanes)
        put_split(jnp.where(is_even, odd, even) * inverse, high.at[number], low.at[number], 0)
        put_split(jnp.where(is_even, even, odd) * inverse, high.at[number], low.at[number], 3)
        for x in range(2):
            put_split(forcing_ref[first + number, :, x].reshape(size, lanes) * inverse, high.at[number], low.at[number], x + 1)
        applied = apply_pair(high.at[number], low.at[number], packed, 0)
        for x in range(2):
            load = forcing_ref[first + number, :, x].reshape(size, lanes)
            value = load * inverse + (load - applied[x]) * inverse
            settled_ref[number, :, x] = value.reshape(3, rows, lanes)


def first_kernel(own, halo, groups, slot_dev, slot_ref, coupling_ref, fields_ref, image_ref, next_ref, modes):
    fields_window(own, halo, fields_ref, modes)
    source = jnp.int32(0)
    for group in range(groups):
        source = jnp.where(slot_ref[group * slot_dev] >= 0, group, source)
    rows = next_ref.shape[1]
    image = image_ref[source, :rows]
    for dim in range(DIMS):
        next_ref[dim] = -(modes[dim] * coupling_ref[dim, dim + 1]) * image


def level_kernel(level, own, halo, rows, caps, starts, base, slot_dev, slot_ref, coupling_ref, stencil_ref, load_hbm, even_hbm, odd_hbm, fields_ref, image_ref, *refs):
    load_ref, even_ref, odd_ref, semaphores, modes, packed, packed2, images, in_place, out_place, ext, ext2, high, low, high2, low2 = refs[-16:]
    olds = refs[:1] if level > 1 else ()
    copies = start_copies((load_hbm, even_hbm, odd_hbm), (load_ref, even_ref, odd_ref), semaphores)
    settled_ref, next_ref, *pieces = refs[len(olds) : -16]
    groups = lax.axis_size("terms")
    group = lax.axis_index("terms")
    lanes = load_ref.shape[2]
    width = own + 2 * halo
    height, height2, height3 = eight(width), eight(width - 2), eight(width - 4)
    next_width = width - 4
    offset = sum(caps[1:level])
    stride = offset + caps[level]
    places(in_place, starts[level], caps[level], caps[level], 0, groups, slot_dev, slot_ref)
    places(out_place, starts[level], caps[level], stride, offset, groups, slot_dev, slot_ref)
    inverse = inverse_pivots(stencil_ref, height, lanes)
    inverse2 = inverse_pivots(stencil_ref, height2, lanes)
    place = lax.broadcasted_iota(jnp.int32, (3 * height2, lanes), 0) % height2 + (own * group - halo + 1)
    inside = ((place >= 0) & (place < rows)).astype(F32)
    is_even, has_lower, has_upper = edge_flags()
    ext[...] = jnp.zeros(ext.shape, F32)
    ext2[...] = jnp.zeros(ext2.shape, F32)
    fill_matrix(1, stencil_ref, packed)
    fill_matrix(1, stencil_ref, packed2)
    fields_window(own, halo - 2, fields_ref, modes)
    for copy in copies:
        copy.wait()
    for old_ref in olds:
        for source in range(groups):
            settled_ref[source * stride : source * stride + offset] = old_ref[source * offset : (source + 1) * offset]

    def plane_of(ref, term, a, x):
        start = (2 * a + x) * width
        return ref[term, start : start + width]

    def terms(step, carry):
        lanes_of = [(lane, step * UNROLL + lane) for lane in range(UNROLL)]
        for lane, term in lanes_of:
            for x in range(6):
                for a in range(3):
                    if 2 <= x < 4:
                        value = plane_of(load_ref, term, a, x - 2)
                    else:
                        even, odd = plane_of(even_ref, term, a, x % 2), plane_of(odd_ref, term, a, x % 2)
                        value = jnp.where(is_even, odd, even) if x < 2 else jnp.where(is_even, even, odd)
                    ext[lane, x, a * height : a * height + width] = value
                    if 1 <= x < 5:
                        ext2[lane, x - 1, a * height2 : a * height2 + width - 2] = value[1 : width - 1]
                put_split(ext[lane, x] * inverse, high.at[lane], low.at[lane], x)
        for lane, term in lanes_of:
            out_slot = out_place[FIRSTS[level] + term]
            for pair in range(2):
                applied = apply_pair(high.at[lane], low.at[lane], packed, 2 * pair)
                for half in range(2):
                    x = 2 * pair + half
                    load = ext2[lane, x]
                    value = (load * inverse2 + (load - applied[half]) * inverse2) * inside
                    if x == 0:
                        value = jnp.where(has_lower, value, 0.0)
                    if x == 3:
                        value = jnp.where(has_upper, value, 0.0)
                    if 1 <= x < 3:
                        for a in range(3):
                            plane = 2 * a + x - 1
                            begin = a * height2 + halo - 1
                            settled_ref[out_slot, plane * own : (plane + 1) * own] = value[begin : begin + own]
                    put_split(value, high2.at[lane], low2.at[lane], x)
        for lane, term in lanes_of:
            in_slot = in_place[FIRSTS[level] + term]
            applied = apply_pair(high2.at[lane], low2.at[lane], packed2, 0)
            for a in range(3):
                for x in range(2):
                    begin = (2 * a + x) * next_width
                    part = pl.ds(begin, next_width)
                    images[term, part] = applied[x][a * height3 : a * height3 + next_width] + image_ref[in_slot, pl.ds(base + begin, next_width)]
        return carry

    lax.fori_loop(0, COUNTS[level] // UNROLL, terms, 0)

    for child in range(COUNTS[level + 1]):
        number = FIRSTS[level + 1] + child
        total = 0.0
        for dim, parent in zip(LINK_DIMS[number], LINK_PARENTS[number], strict=True):
            if parent >= 0:
                total = total - (modes[int(dim)] * coupling_ref[int(dim), number]) * images[int(parent) - FIRSTS[level]]
        next_ref[child] = total
    if pieces:

        def cut(pair, carry):
            for lane in range(2):
                for a in range(3):
                    layers = [next_ref[2 * pair + lane, (2 * a + x) * next_width : (2 * a + x + 1) * next_width] for x in range(2)]
                    begin = (3 * lane + a) * next_width
                    pieces[0][pair, begin : begin + next_width] = jnp.where(is_even, layers[1], layers[0])
                    pieces[1][pair, begin : begin + next_width] = jnp.where(is_even, layers[0], layers[1])
            return carry

        lax.fori_loop(0, COUNTS[level + 1] // 2, cut, 0)


def last_kernel(own, caps, starts, slot_dev, slot_ref, stencil_ref, load_hbm, even_hbm, odd_hbm, settled_ref, load_ref, even_ref, odd_ref, semaphores, packed, place, ext, high, low):
    groups = lax.axis_size("terms")
    lanes = load_ref.shape[2]
    width = own + 2
    height, height2 = eight(width), eight(own)
    places(place, starts[DEGREE], caps[DEGREE], caps[DEGREE], 0, groups, slot_dev, slot_ref)
    inverse = inverse_pivots(stencil_ref, height, lanes)
    is_even = edge_flags()[0]
    copies = start_copies((load_hbm, even_hbm, odd_hbm), (load_ref, even_ref, odd_ref), semaphores)
    ext[...] = jnp.zeros(ext.shape, F32)
    fill_matrix(1, stencil_ref, packed)
    for copy in copies:
        copy.wait()

    def terms(step, carry):
        for lane in range(2 * UNROLL):
            term = step * 2 * UNROLL + lane
            pair = step * UNROLL + lane // 2
            for a in range(3):
                begin = (3 * (lane % 2) + a) * width
                even = even_ref[pair, begin : begin + width]
                odd = odd_ref[pair, begin : begin + width]
                ext[lane, 0, a * height : a * height + width] = jnp.where(is_even, odd, even)
                ext[lane, 3, a * height : a * height + width] = jnp.where(is_even, even, odd)
                for x in range(2):
                    begin = (2 * a + x) * width
                    ext[lane, x + 1, a * height : a * height + width] = load_ref[term, begin : begin + width]
            for x in range(4):
                put_split(ext[lane, x] * inverse, high.at[lane], low.at[lane], x)
        for lane in range(2 * UNROLL):
            term = step * 2 * UNROLL + lane
            applied = apply_pair(high.at[lane], low.at[lane], packed, 0)
            slot = place[FIRSTS[DEGREE] + term]
            for a in range(3):
                scale = inverse[a * height : a * height + own]
                for x in range(2):
                    begin = (2 * a + x) * width + 1
                    load = load_ref[term, begin : begin + own]
                    plane = 2 * a + x
                    settled_ref[slot, plane * own : (plane + 1) * own] = load * scale + (load - applied[x][a * height2 : a * height2 + own]) * scale
        return carry

    lax.fori_loop(0, COUNTS[DEGREE] // (2 * UNROLL), terms, 0)


def assemble_kernel(own, starts, slot_ref, *refs):
    out_ref = refs[-1]
    parts = refs[: DEGREE + 1]
    links = refs[DEGREE + 1 : -1]
    slot_dev, _, _, rows, lanes = out_ref.shape
    groups = rows // own
    first = lax.axis_index("terms") * slot_dev
    out_ref[0] = jnp.where(slot_ref[first] >= 0, parts[0][0], 0.0)
    for level in range(1, DEGREE + 1):
        ref = links[level // DEGREE]
        offset = starts[level] - starts[1] if level < DEGREE else 0
        for slot in range(parts[level].shape[0]):
            filled = slot_ref[first + starts[level] + slot] >= 0
            for plane in range(6):
                begin = ((offset + slot) * 6 + plane) * own
                value = jnp.concatenate([ref[group, begin : begin + own] for group in range(groups)], axis=0)
                value = value + parts[level][slot, plane // 2, plane % 2]
                out_ref[starts[level] + slot, plane // 2, plane % 2] = jnp.where(filled, value, 0.0)


def call(kernel, out_shape, specs, scratch, operands, name, flops=0, megabytes=12):
    single = not isinstance(out_shape, list)
    return pl.pallas_call(
        kernel,
        out_shape=out_shape,
        in_specs=specs,
        out_specs=VMEM if single else [VMEM] * len(out_shape),
        scratch_shapes=scratch,
        compiler_params=pltpu.CompilerParams(vmem_limit_bytes=megabytes * 2**20),
        cost_estimate=pl.CostEstimate(flops=flops, bytes_accessed=sum(4 * math.prod(o.shape) for o in operands), transcendentals=0),
        name=name,
    )(*operands)


def beside(array, axis):
    count = lax.axis_size(axis)
    even = [(i, i ^ 1) for i in range(count)]
    odd = [(i, ((i + 1) ^ 1) - 1) for i in range(1, count - 1)]
    return lax.ppermute(array[0], axis, even), lax.ppermute(array[1], axis, odd)


def exchange(blocks):
    return lax.all_to_all(blocks, "terms", 0, 0, tiled=True)


def on_device(forcing, stencil, fields, coupling, slot_term):
    groups = lax.axis_size("terms")
    slot_dev = forcing.shape[0]
    caps = [(count + groups - 1) // groups for count in COUNTS]
    starts = [sum(caps[:level]) for level in range(DEGREE + 1)]
    rows, lanes = forcing.shape[3:]
    field = forcing.shape[1:]
    own = rows // groups
    halos = [None] + [2 * (DEGREE - level) + 1 for level in range(1, DEGREE + 1)]
    widths = [None] + [own + 2 * halo for halo in halos[1:]]
    strides = [None] + [eight(6 * width) for width in widths[1:]]

    def array(*shape):
        return jax.ShapeDtypeStruct(shape, F32)

    taps = jnp.transpose(stencil, (1, 2, 0))
    weights = coupling.T
    whole = call(matrix_kernel, jax.ShapeDtypeStruct((9 * rows, 27 * rows), BF16), [SMEM], [], [taps], "matrix")

    def splits(lead, layers, size):
        return [pltpu.VMEM((lead, layers, size, lanes), BF16)] * 2

    def own_part(slots, beside_pair, base, levels):
        layout, row = [], 0
        for level in levels:
            for _ in range(caps[level]):
                layout.append((halos[level + 1], row))
                row += strides[level + 1]
        count = len(layout)
        size = 3 * rows
        return call(
            functools.partial(own_kernel, own, starts[levels[0]] - base, layout),
            [pltpu.HBM((count, *field), F32), pltpu.HBM((groups, row, lanes), F32)],
            [SMEM] + [VMEM] * 4,
            [pltpu.VMEM((count, 2, size, lanes), F32)] + splits(count, 6, size) + splits(count, 4, size),
            [taps, whole, slots, *beside_pair],
            "own",
            count * 3 * 2 * 27 * size * size * 256,
        )

    front = forcing[: starts[2]]
    part01, packed = own_part(front, beside((front, front), "space"), 0, (0, 1))
    packed, forcing = lax.optimization_barrier((packed, forcing))
    back = forcing[starts[2] : starts[4]]
    back_pair = beside((back, back), "space")
    part2, packed2 = own_part(back, back_pair, starts[2], (2,))
    part3, packed3 = own_part(back, back_pair, starts[2], (3,))
    is_even = lax.axis_index("space") % 2 == 0
    layers = [forcing[starts[4] :, :, x] for x in range(2)]
    pieces = (jnp.where(is_even, layers[1], layers[0]), jnp.where(is_even, layers[0], layers[1]))
    front_images, packed2, packed3, last_pair = lax.optimization_barrier((exchange(packed), packed2, packed3, beside(pieces, "space")))
    part4 = call(
        functools.partial(own_last_kernel, starts[4]),
        pltpu.HBM((caps[4], *field), F32),
        [SMEM] + [VMEM] * 4,
        splits(caps[4], 4, 3 * rows),
        [taps, whole, forcing, *last_pair],
        "own_last",
        caps[4] * 2 * 27 * 9 * rows * rows * 256,
    )
    load = call(
        functools.partial(first_kernel, own, halos[1], groups, slot_dev),
        pltpu.HBM((DIMS, strides[1], lanes), F32),
        [SMEM] * 2 + [VMEM] * 2,
        [pltpu.VMEM((DIMS, strides[1], lanes), F32)],
        [slot_term, weights, fields, front_images],
        "first",
    )
    images = [None, front_images, None, None]
    waiting = [None, packed2, packed3]
    table = pltpu.SMEM((128,), jnp.int32)
    settled = []
    for level in range(1, DEGREE):
        height, height2 = eight(widths[level]), eight(widths[level] - 2)
        base = strides[1] if level == 1 else 0
        image = images[level].reshape(groups * (1 if level == 1 else caps[level]), -1, lanes)
        olds = settled
        total = sum(caps[1 : level + 1])
        shapes = [pltpu.HBM((groups * total, 6 * own, lanes), F32), pltpu.HBM((COUNTS[level + 1], strides[level + 1], lanes), F32)]
        if level == DEGREE - 1:
            shapes += [pltpu.HBM((COUNTS[DEGREE] // 2, 6 * widths[DEGREE], lanes), F32)] * 2
        size, size2 = 3 * height, 3 * height2
        even, odd = beside((load, load), "space")
        if level < 3:
            even, block = lax.optimization_barrier((even, waiting[level]))
            images[level + 1] = exchange(block)
        result, load, *pieces = call(
            functools.partial(level_kernel, level, own, halos[level], rows, caps, starts, base, slot_dev),
            shapes,
            [SMEM] * 3 + [HBM] * 3 + [VMEM] * (2 + len(olds)),
            [pltpu.VMEM((COUNTS[level], strides[level], lanes), F32)] * 3
            + [pltpu.SemaphoreType.DMA((3,)), pltpu.VMEM((DIMS, strides[level + 1], lanes), F32)]
            + [pltpu.VMEM((3 * size2, 9 * size), BF16), pltpu.VMEM((9 * eight(widths[level] - 4), 9 * size2), BF16)]
            + [pltpu.VMEM((COUNTS[level], strides[level + 1], lanes), F32), table, table]
            + [pltpu.VMEM((UNROLL, 6, size, lanes), F32), pltpu.VMEM((UNROLL, 4, size2, lanes), F32)]
            + splits(UNROLL, 6, size)
            + splits(UNROLL, 4, size2),
            [slot_term, weights, taps, load, even, odd, fields, image, *olds],
            "level",
            COUNTS[level] * 2 * 27 * size2 * (2 * size + size2) * 256,
            60,
        )
        settled = [result]
    middle = exchange(result.reshape(groups, -1, lanes))
    even, odd = beside(pieces, "space")
    height, height2 = eight(widths[DEGREE]), eight(own)
    result = call(
        functools.partial(last_kernel, own, caps, starts, slot_dev),
        pltpu.HBM((groups * caps[DEGREE], 6 * own, lanes), F32),
        [SMEM] * 2 + [HBM] * 3,
        [pltpu.VMEM((COUNTS[DEGREE], strides[DEGREE], lanes), F32)]
        + [pltpu.VMEM((COUNTS[DEGREE] // 2, 6 * widths[DEGREE], lanes), F32)] * 2
        + [pltpu.SemaphoreType.DMA((3,)), pltpu.VMEM((9 * height2, 27 * height), BF16), table, pltpu.VMEM((2 * UNROLL, 4, 3 * height, lanes), F32)] + splits(2 * UNROLL, 4, 3 * height),
        [slot_term, taps, load, even, odd],
        "level_last",
        COUNTS[DEGREE] * 2 * 27 * 9 * height * height2 * 256,
        60,
    )
    result, middle = lax.optimization_barrier((result, middle))
    final = exchange(result.reshape(groups, -1, lanes))
    return call(
        functools.partial(assemble_kernel, own, starts),
        array(*forcing.shape),
        [SMEM] + [VMEM] * (DEGREE + 3),
        [],
        [slot_term, part01[:1], part01[1:], part2, part3, part4, middle, final],
        "assemble",
    )


def solution(mesh):
    return jax.shard_map(
        on_device,
        mesh=mesh,
        in_specs=(
            P("terms", None, "space", None, None),
            P(),
            P(None, "space", None, None),
            P(),
            P(),
        ),
        out_specs=P("terms", None, "space", None, None),
        check_vma=False,
    )
```

```python
import functools
import math

import jax
import jax.numpy as jnp
import numpy as np
from jax import lax
from jax.experimental import pallas as pl
from jax.experimental.pallas import tpu as pltpu
from jax.sharding import PartitionSpec as P

DIMS = 5
DEGREE = 4
UNROLL = 5
F32 = jnp.float32
BF16 = jnp.bfloat16
ANY = pl.BlockSpec(memory_space=pl.ANY)
VMEM = pl.BlockSpec(memory_space=pltpu.VMEM)
HBM = pl.BlockSpec(memory_space=pltpu.HBM)
SMEM = pl.BlockSpec(memory_space=pltpu.SMEM)


def compositions(total, pieces_left):
    if pieces_left == 1:
        return [[total]]
    result = []
    for leading in range(total, -1, -1):
        for remainder in compositions(total - leading, pieces_left - 1):
            result.append([leading] + remainder)
    return result


def chaos_links():
    indices = []
    for level in range(DEGREE + 1):
        indices.extend(compositions(level, DIMS))
    lookup = {tuple(vector): number for number, vector in enumerate(indices)}
    dims = np.zeros((len(indices), DEGREE), np.int32)
    parents = np.full((len(indices), DEGREE), -1, np.int32)
    for number, vector in enumerate(indices):
        place = 0
        for dim in range(DIMS):
            if vector[dim] > 0:
                lowered = list(vector)
                lowered[dim] -= 1
                dims[number, place] = dim
                parents[number, place] = lookup[tuple(lowered)]
                place += 1
    return dims, parents


LINK_DIMS, LINK_PARENTS = chaos_links()
COUNTS = [math.comb(level + DIMS - 1, DIMS - 1) for level in range(DEGREE + 1)]
FIRSTS = [sum(COUNTS[:level]) for level in range(DEGREE + 1)]


def matrix_kernel(stencil_ref, packed_ref):
    fill_matrix(0, stencil_ref, packed_ref)


def fill_matrix(shift, stencil_ref, packed_ref):
    size = packed_ref.shape[1] // 3
    rows = size // 9
    out_rows = packed_ref.shape[0] // 9
    lane = lax.broadcasted_iota(jnp.int32, (out_rows, size), 1)
    step = lane % rows - lax.broadcasted_iota(jnp.int32, (out_rows, size), 0) + (1 - shift)
    column = lane // rows
    for oz in range(3):
        for a in range(3):
            block = jnp.zeros((out_rows, size), F32)
            for oy in range(3):
                taps = jnp.zeros((out_rows, size), F32)
                for ox in range(3):
                    for b in range(3):
                        taps = jnp.where(column == 3 * ox + b, stencil_ref[a, b, 9 * ox + 3 * oy + oz], taps)
                block = jnp.where(step == oy, taps, block)
            high = block.astype(BF16)
            place = pl.ds((3 * oz + a) * out_rows, out_rows)
            packed_ref[place, :size] = high
            packed_ref[place, size : 2 * size] = high
            packed_ref[place, 2 * size :] = (block - high.astype(F32)).astype(BF16)


def put_split(value, high_ref, low_ref, place):
    high = value.astype(BF16)
    high_ref[place] = high
    low_ref[place] = (value - high.astype(F32)).astype(BF16)


def apply_pair(high_ref, low_ref, packed_ref, place):
    def window(ref):
        return [jnp.concatenate([ref[place + k], ref[place + k + 1]], axis=1) for k in range(3)]

    high = window(high_ref)
    operand = jnp.concatenate(high + window(low_ref) + high, axis=0)
    product = jnp.dot(packed_ref[...], operand, preferred_element_type=F32)
    lanes = high_ref.shape[2]
    size = packed_ref.shape[0] // 3
    lane = lax.broadcasted_iota(jnp.int32, (size, lanes), 1)
    results = []
    for half in range(2):
        block = product[:, half * lanes : (half + 1) * lanes]
        before = pltpu.roll(block[:size], 1, 1)
        after = pltpu.roll(block[2 * size :], lanes - 1, 1)
        results.append(block[size : 2 * size] + jnp.where(lane > 0, before, 0.0) + jnp.where(lane < lanes - 1, after, 0.0))
    return results


def start_copies(sources, targets, semaphores):
    copies = [pltpu.make_async_copy(source, target, semaphores.at[i]) for i, (source, target) in enumerate(zip(sources, targets, strict=True))]
    for copy in copies:
        copy.start()
    return copies


def eight(rows):
    return (rows + 7) // 8 * 8


def inverse_pivots(stencil_ref, rows, lanes):
    return jnp.concatenate([1.0 / jnp.full((rows, lanes), stencil_ref[a, a, 13], F32) for a in range(3)], axis=0)


def edge_flags():
    slab = lax.axis_index("space")
    return slab % 2 == 0, slab > 0, slab < lax.axis_size("space") - 1


def window(start, width, rows):
    first = max(start, 0)
    last = min(start + width, rows)
    return first, first - start, last - first


def fields_window(own, halo, layers, fields_ref, out):
    group = lax.axis_index("terms")
    rows, lanes = fields_ref.shape[2:]
    width = own + 2 * halo
    for case in range(lax.axis_size("terms")):

        @pl.when(group == case)
        def _():
            first, place, length = window(own * case - halo, width, rows)
            for dim in range(DIMS):
                for plane in range(3 * len(layers)):
                    base = plane * width
                    if place:
                        out[dim, base : base + place] = jnp.zeros((place, lanes), F32)
                    out[dim, base + place : base + place + length] = fields_ref[dim, layers[plane % len(layers)], first : first + length]
                    if place + length < width:
                        out[dim, base + place + length : base + width] = jnp.zeros((width - place - length, lanes), F32)


def link_sums(level, coupling_ref, modes, image_of, out):
    for child in range(COUNTS[level]):
        number = FIRSTS[level] + child
        total = 0.0
        for dim, parent in zip(LINK_DIMS[number], LINK_PARENTS[number], strict=True):
            if parent >= 0:
                total = total - (modes[int(dim)] * coupling_ref[int(dim), number]) * image_of(int(parent) - FIRSTS[level - 1])
        out[child] = total


def places(place, start, cap, stride, offset, groups, slot_dev, slot_ref):
    for source in range(groups):
        for slot in range(cap):
            term = slot_ref[source * slot_dev + start + slot]
            place[jnp.where(term >= 0, term, 127)] = source * stride + offset + slot


def own_kernel(own, first, layout, stencil_ref, packed, forcing_ref, even_ref, odd_ref, settled_ref, out_ref, image, high, low, high2, low2):
    rows, lanes = forcing_ref.shape[3:]
    size = 3 * rows
    groups = out_ref.shape[0]
    inverse = inverse_pivots(stencil_ref, rows, lanes)
    is_even, has_lower, has_upper = edge_flags()

    def load(number, x):
        slot = first + number
        if 2 <= x < 4:
            return forcing_ref[slot, :, x - 2].reshape(size, lanes)
        even = even_ref[slot, :, x % 2].reshape(size, lanes)
        odd = odd_ref[slot, :, x % 2].reshape(size, lanes)
        return jnp.where(is_even, odd, even) if x < 2 else jnp.where(is_even, even, odd)

    for number in range(len(layout)):
        for x in range(6):
            put_split(load(number, x) * inverse, high.at[number], low.at[number], x)
    for number in range(len(layout)):
        for pair in range(2):
            applied = apply_pair(high.at[number], low.at[number], packed, 2 * pair)
            for half in range(2):
                x = 2 * pair + half + 1
                load_x = load(number, x)
                value = load_x * inverse + (load_x - applied[half]) * inverse
                if x == 1:
                    value = jnp.where(has_lower, value, 0.0)
                if x == 4:
                    value = jnp.where(has_upper, value, 0.0)
                if 2 <= x < 4:
                    settled_ref[number, :, x - 2] = value.reshape(3, rows, lanes)
                put_split(value, high2.at[number], low2.at[number], x - 1)
    for number, (halo, row) in enumerate(layout):
        applied = apply_pair(high2.at[number], low2.at[number], packed, 0)
        for x in range(2):
            image[number, x] = applied[x]
        width = own + 2 * halo
        for group in range(groups):
            begin, place, length = window(own * group - halo, width, rows)
            for plane in range(6):
                target = row + plane * width
                start = plane // 2 * rows + begin
                if place:
                    out_ref[group, target : target + place] = jnp.zeros((place, lanes), F32)
                out_ref[group, target + place : target + place + length] = image[number, plane % 2, start : start + length]
                if place + length < width:
                    out_ref[group, target + place + length : target + width] = jnp.zeros((width - place - length, lanes), F32)


def own_last_kernel(first, stencil_ref, packed, forcing_ref, even_ref, odd_ref, settled_ref, high, low):
    rows, lanes = forcing_ref.shape[3:]
    size = 3 * rows
    inverse = inverse_pivots(stencil_ref, rows, lanes)
    is_even = edge_flags()[0]
    for number in range(settled_ref.shape[0]):
        even = even_ref[number].reshape(size, lanes)
        odd = odd_ref[number].reshape(size, lanes)
        put_split(jnp.where(is_even, odd, even) * inverse, high.at[number], low.at[number], 0)
        put_split(jnp.where(is_even, even, odd) * inverse, high.at[number], low.at[number], 3)
        for x in range(2):
            put_split(forcing_ref[first + number, :, x].reshape(size, lanes) * inverse, high.at[number], low.at[number], x + 1)
        applied = apply_pair(high.at[number], low.at[number], packed, 0)
        for x in range(2):
            load = forcing_ref[first + number, :, x].reshape(size, lanes)
            value = load * inverse + (load - applied[x]) * inverse
            settled_ref[number, :, x] = value.reshape(3, rows, lanes)


def first_kernel(groups, slot_dev, slot_ref, image_ref, out_ref):
    source = jnp.int32(0)
    for group in range(groups):
        source = jnp.where(slot_ref[group * slot_dev] >= 0, group, source)
    out_ref[0] = image_ref[source, : out_ref.shape[1]]


def level_kernel(level, own, halo, rows, caps, starts, base, slot_dev, slot_ref, coupling_ref, stencil_ref, own_hbm, even_hbm, odd_hbm, fields_hbm, fields_even, fields_odd, image_ref, *refs):
    slabs, fields, semaphores, modes, loads, packed, packed2, in_place, out_place, ext, ext2, high, low, high2, low2 = refs[-15:]
    olds = refs[:1] if level > 1 else ()
    is_even, has_lower, has_upper = edge_flags()
    side = jnp.where(is_even, 2, 0)
    places_of = (1, side, 2 - side)
    copies = start_copies(
        (own_hbm, even_hbm, odd_hbm, fields_hbm, fields_even, fields_odd),
        [slabs.at[place] for place in places_of] + [fields.at[place] for place in places_of],
        semaphores,
    )
    settled_ref, images, *pieces = refs[len(olds) : -15]
    groups = lax.axis_size("terms")
    group = lax.axis_index("terms")
    lanes = images.shape[2]
    width = own + 2 * halo
    height, height2, height3 = eight(width), eight(width - 2), eight(width - 4)
    next_width = width - 4
    offset = sum(caps[1:level])
    stride = offset + caps[level]
    places(in_place, starts[level], caps[level], caps[level], 0, groups, slot_dev, slot_ref)
    places(out_place, starts[level], caps[level], stride, offset, groups, slot_dev, slot_ref)
    inverse = inverse_pivots(stencil_ref, height, lanes)
    inverse2 = inverse_pivots(stencil_ref, height2, lanes)
    place = lax.broadcasted_iota(jnp.int32, (3 * height2, lanes), 0) % height2 + (own * group - halo + 1)
    inside = ((place >= 0) & (place < rows)).astype(F32)
    ext[...] = jnp.zeros(ext.shape, F32)
    ext2[...] = jnp.zeros(ext2.shape, F32)
    fill_matrix(1, stencil_ref, packed)
    fill_matrix(1, stencil_ref, packed2)
    for copy in copies:
        copy.wait()
    for slab in range(3):
        fields_window(own, halo, (0, 1), fields.at[slab], modes.at[slab])
        link_sums(level, coupling_ref, modes.at[slab], lambda parent, slab=slab: slabs[slab, parent], loads.at[slab])
    for old_ref in olds:
        for source in range(groups):
            settled_ref[source * stride : source * stride + offset] = old_ref[source * offset : (source + 1) * offset]

    def terms(step, carry):
        lanes_of = [(lane, step * UNROLL + lane) for lane in range(UNROLL)]
        for lane, term in lanes_of:
            for x in range(6):
                for a in range(3):
                    start = (2 * a + x % 2) * width
                    value = loads[x // 2, term, start : start + width]
                    ext[lane, x, a * height : a * height + width] = value
                    if 1 <= x < 5:
                        ext2[lane, x - 1, a * height2 : a * height2 + width - 2] = value[1 : width - 1]
                put_split(ext[lane, x] * inverse, high.at[lane], low.at[lane], x)
        for lane, term in lanes_of:
            out_slot = out_place[FIRSTS[level] + term]
            for pair in range(2):
                applied = apply_pair(high.at[lane], low.at[lane], packed, 2 * pair)
                for half in range(2):
                    x = 2 * pair + half
                    load = ext2[lane, x]
                    value = (load * inverse2 + (load - applied[half]) * inverse2) * inside
                    if x == 0:
                        value = jnp.where(has_lower, value, 0.0)
                    if x == 3:
                        value = jnp.where(has_upper, value, 0.0)
                    if 1 <= x < 3:
                        for a in range(3):
                            plane = 2 * a + x - 1
                            begin = a * height2 + halo - 1
                            settled_ref[out_slot, plane * own : (plane + 1) * own] = value[begin : begin + own]
                    put_split(value, high2.at[lane], low2.at[lane], x)
        for lane, term in lanes_of:
            in_slot = in_place[FIRSTS[level] + term]
            applied = apply_pair(high2.at[lane], low2.at[lane], packed2, 0)
            for a in range(3):
                for x in range(2):
                    begin = (2 * a + x) * next_width
                    part = pl.ds(begin, next_width)
                    images[term, part] = applied[x][a * height3 : a * height3 + next_width] + image_ref[in_slot, pl.ds(base + begin, next_width)]
        return carry

    lax.fori_loop(0, COUNTS[level] // UNROLL, terms, 0)

    if pieces:
        for term in range(COUNTS[level]):
            for a in range(3):
                layers = [images[term, (2 * a + x) * next_width : (2 * a + x + 1) * next_width] for x in range(2)]
                begin = (3 * (term % 4) + a) * next_width
                pieces[0][term // 4, begin : begin + next_width] = jnp.where(is_even, layers[1], layers[0])
                pieces[1][term // 4, begin : begin + next_width] = jnp.where(is_even, layers[0], layers[1])


def last_kernel(own, caps, starts, slot_dev, slot_ref, coupling_ref, stencil_ref, own_hbm, even_hbm, odd_hbm, fields_hbm, fields_even, fields_odd, settled_ref, images, sides, fields, semaphores, modes, side_modes, loads, side_loads, packed, place, ext, high, low):
    groups = lax.axis_size("terms")
    lanes = settled_ref.shape[2]
    width = own + 2
    height, height2 = eight(width), eight(own)
    side = jnp.where(edge_flags()[0], 1, 0)
    copies = start_copies(
        (own_hbm, even_hbm, odd_hbm, fields_hbm, fields_even, fields_odd),
        (images, sides.at[side], sides.at[1 - side], fields.at[2], fields.at[side], fields.at[1 - side]),
        semaphores,
    )
    places(place, starts[DEGREE], caps[DEGREE], caps[DEGREE], 0, groups, slot_dev, slot_ref)
    inverse = inverse_pivots(stencil_ref, height, lanes)
    ext[...] = jnp.zeros(ext.shape, F32)
    fill_matrix(1, stencil_ref, packed)
    for copy in copies:
        copy.wait()
    fields_window(own, 1, (0, 1), fields.at[2], modes)
    link_sums(DEGREE, coupling_ref, modes, lambda parent: images[parent], loads)
    for upper in range(2):

        def side_image(parent, upper=upper):
            begin = 3 * (parent % 4) * width
            return sides[upper, parent // 4, begin : begin + 3 * width]

        fields_window(own, 1, (1 - upper,), fields.at[upper], side_modes.at[upper])
        link_sums(DEGREE, coupling_ref, side_modes.at[upper], side_image, side_loads.at[upper])

    def terms(step, carry):
        for lane in range(2 * UNROLL):
            term = step * 2 * UNROLL + lane
            for a in range(3):
                for upper in range(2):
                    ext[lane, 3 * upper, a * height : a * height + width] = side_loads[upper, term, a * width : (a + 1) * width]
                for x in range(2):
                    begin = (2 * a + x) * width
                    ext[lane, x + 1, a * height : a * height + width] = loads[term, begin : begin + width]
            for x in range(4):
                put_split(ext[lane, x] * inverse, high.at[lane], low.at[lane], x)
        for lane in range(2 * UNROLL):
            term = step * 2 * UNROLL + lane
            applied = apply_pair(high.at[lane], low.at[lane], packed, 0)
            slot = place[FIRSTS[DEGREE] + term]
            for a in range(3):
                scale = inverse[a * height : a * height + own]
                for x in range(2):
                    begin = (2 * a + x) * width + 1
                    load = loads[term, begin : begin + own]
                    plane = 2 * a + x
                    settled_ref[slot, plane * own : (plane + 1) * own] = load * scale + (load - applied[x][a * height2 : a * height2 + own]) * scale
        return carry

    lax.fori_loop(0, COUNTS[DEGREE] // (2 * UNROLL), terms, 0)


def assemble_kernel(own, start, slot_ref, *refs):
    *parts, links_ref, out_ref = refs
    slot_dev, _, _, rows, lanes = out_ref.shape
    groups = rows // own
    first = lax.axis_index("terms") * slot_dev
    out_ref[0] = jnp.where(slot_ref[first] >= 0, parts[0][0], 0.0)
    begin = 1
    for number, part in enumerate(parts):
        skip = 1 if number == 0 else 0
        for slot in range(part.shape[0] - skip):
            filled = slot_ref[first + begin] >= 0
            for plane in range(6):
                place = ((begin - 1) * 6 + plane) * own
                value = part[skip + slot, plane // 2, plane % 2]
                if begin < start:
                    value = value + jnp.concatenate([links_ref[group, place : place + own] for group in range(groups)], axis=0)
                out_ref[begin, plane // 2, plane % 2] = jnp.where(filled, value, 0.0)
            begin += 1


def finish_kernel(own, start, slot_ref, partial_ref, links_hbm, out_ref, block, links_ref, semaphores):
    slot_dev = out_ref.shape[0]
    rows = out_ref.shape[3]
    count = slot_dev - start
    groups = rows // own
    first = lax.axis_index("terms") * slot_dev + start
    copies = start_copies([links_hbm, *[partial_ref.at[start + slot] for slot in range(count)]], [links_ref, *[block.at[slot] for slot in range(count)]], semaphores)
    copies.pop(0).wait()
    back = [pltpu.make_async_copy(block.at[slot], out_ref.at[start + slot], semaphores.at[1 + slot]) for slot in range(count)]
    for slot in range(count):
        copies[slot].wait()
        filled = slot_ref[first + slot] >= 0
        for plane in range(6):
            place = (slot * 6 + plane) * own
            value = jnp.concatenate([links_ref[group, place : place + own] for group in range(groups)], axis=0)
            block[slot, plane // 2, plane % 2] += jnp.where(filled, value, 0.0)
        back[slot].start()
    for copy in back:
        copy.wait()


def call(kernel, out_shape, specs, scratch, operands, name, flops=0, megabytes=12):
    single = not isinstance(out_shape, list)
    return pl.pallas_call(
        kernel,
        out_shape=out_shape,
        in_specs=specs,
        out_specs=VMEM if single else [VMEM] * len(out_shape),
        scratch_shapes=scratch,
        compiler_params=pltpu.CompilerParams(vmem_limit_bytes=megabytes * 2**20),
        cost_estimate=pl.CostEstimate(flops=flops, bytes_accessed=sum(4 * math.prod(o.shape) for o in operands), transcendentals=0),
        name=name,
    )(*operands)


def beside(array, axis):
    count = lax.axis_size(axis)
    even = [(i, i ^ 1) for i in range(count)]
    odd = [(i, ((i + 1) ^ 1) - 1) for i in range(1, count - 1)]
    return lax.ppermute(array[0], axis, even), lax.ppermute(array[1], axis, odd)


def exchange(blocks):
    return lax.all_to_all(blocks, "terms", 0, 0, tiled=True)


def on_device(forcing, stencil, fields, coupling, slot_term):
    groups = lax.axis_size("terms")
    slot_dev = forcing.shape[0]
    caps = [(count + groups - 1) // groups for count in COUNTS]
    starts = [sum(caps[:level]) for level in range(DEGREE + 1)]
    rows, lanes = forcing.shape[3:]
    field = forcing.shape[1:]
    own = rows // groups
    halos = [None] + [2 * (DEGREE - level) + 1 for level in range(1, DEGREE + 1)]
    widths = [None] + [own + 2 * halo for halo in halos[1:]]
    strides = [None] + [eight(6 * width) for width in widths[1:]]

    def array(*shape):
        return jax.ShapeDtypeStruct(shape, F32)

    taps = jnp.transpose(stencil, (1, 2, 0))
    weights = coupling.T
    whole = call(matrix_kernel, jax.ShapeDtypeStruct((9 * rows, 27 * rows), BF16), [SMEM], [], [taps], "matrix")

    def splits(lead, layers, size):
        return [pltpu.VMEM((lead, layers, size, lanes), BF16)] * 2

    def own_part(slots, beside_pair, base, levels):
        layout, row = [], 0
        for level in levels:
            for _ in range(caps[level]):
                layout.append((halos[level + 1], row))
                row += strides[level + 1]
        count = len(layout)
        size = 3 * rows
        return call(
            functools.partial(own_kernel, own, starts[levels[0]] - base, layout),
            [pltpu.HBM((count, *field), F32), pltpu.HBM((groups, row, lanes), F32)],
            [SMEM] + [VMEM] * 4,
            [pltpu.VMEM((count, 2, size, lanes), F32)] + splits(count, 6, size) + splits(count, 4, size),
            [taps, whole, slots, *beside_pair],
            "own",
            count * 3 * 2 * 27 * size * size * 256,
        )

    front = forcing[: starts[2]]
    part01, packed = own_part(front, beside((front, front), "space"), 0, (0, 1))
    packed, forcing, fields = lax.optimization_barrier((packed, forcing, fields))
    back2, back3 = forcing[starts[2] : starts[3]], forcing[starts[3] : starts[4]]
    part2, packed2 = own_part(back2, beside((back2, back2), "space"), starts[2], (2,))
    part3, packed3 = own_part(back3, beside((back3, back3), "space"), starts[3], (3,))
    fields_pair = beside((fields, fields), "space")
    is_even = lax.axis_index("space") % 2 == 0
    layers = [forcing[starts[4] :, :, x] for x in range(2)]
    borders = (jnp.where(is_even, layers[1], layers[0]), jnp.where(is_even, layers[0], layers[1]))
    front_images, packed2, packed3, fields_pair = lax.optimization_barrier((exchange(packed), packed2, packed3, fields_pair))
    def own_last(pair):
        return call(
            functools.partial(own_last_kernel, starts[4]),
            pltpu.HBM((caps[4], *field), F32),
            [SMEM] + [VMEM] * 4,
            splits(caps[4], 4, 3 * rows),
            [taps, whole, forcing, *pair],
            "own_last",
            caps[4] * 2 * 27 * 9 * rows * rows * 256,
        )

    image = call(
        functools.partial(first_kernel, groups, slot_dev),
        pltpu.HBM((1, strides[1], lanes), F32),
        [SMEM, VMEM],
        [],
        [slot_term, front_images],
        "first",
    )
    arrived = [None, front_images, exchange(packed2), None]
    table = pltpu.SMEM((128,), jnp.int32)
    settled = []
    for level in range(1, DEGREE):
        height, height2 = eight(widths[level]), eight(widths[level] - 2)
        base = strides[1] if level == 1 else 0
        part = arrived[level].reshape(groups * (1 if level == 1 else caps[level]), -1, lanes)
        olds = settled
        total = sum(caps[1 : level + 1])
        shapes = [pltpu.HBM((groups * total, 6 * own, lanes), F32), pltpu.HBM((COUNTS[level], strides[level + 1], lanes), F32)]
        if level == DEGREE - 1:
            shapes += [pltpu.HBM(((COUNTS[level] + 3) // 4, 12 * widths[DEGREE], lanes), F32)] * 2
        size, size2 = 3 * height, 3 * height2
        even, odd = beside((image, image), "space")
        if level == 2:
            even, packed3 = lax.optimization_barrier((even, packed3))
            arrived[3] = exchange(packed3)
        result, image, *pieces = call(
            functools.partial(level_kernel, level, own, halos[level], rows, caps, starts, base, slot_dev),
            shapes,
            [SMEM] * 3 + [HBM] * 6 + [VMEM] * (1 + len(olds)),
            [pltpu.VMEM((3, COUNTS[level - 1], strides[level], lanes), F32), pltpu.VMEM((3, *fields.shape), F32), pltpu.SemaphoreType.DMA((6,))]
            + [pltpu.VMEM((3, DIMS, strides[level], lanes), F32), pltpu.VMEM((3, COUNTS[level], strides[level], lanes), F32)]
            + [pltpu.VMEM((3 * size2, 9 * size), BF16), pltpu.VMEM((9 * eight(widths[level] - 4), 9 * size2), BF16)]
            + [table, table]
            + [pltpu.VMEM((UNROLL, 6, size, lanes), F32), pltpu.VMEM((UNROLL, 4, size2, lanes), F32)]
            + splits(UNROLL, 6, size)
            + splits(UNROLL, 4, size2),
            [slot_term, weights, taps, image, even, odd, fields, *fields_pair, part, *olds],
            "level",
            (1 if level == 1 else 30) * COUNTS[level] * 2 * 27 * size2 * (2 * size + size2) * 256,
            63,
        )
        settled = [result]
    middle = exchange(result.reshape(groups, -1, lanes))
    even, odd = beside(pieces, "space")
    even, odd, borders = lax.optimization_barrier((even, odd, borders))
    part4 = own_last(beside(borders, "space"))
    height, height2 = eight(widths[DEGREE]), eight(own)
    result = call(
        functools.partial(last_kernel, own, caps, starts, slot_dev),
        pltpu.HBM((groups * caps[DEGREE], 6 * own, lanes), F32),
        [SMEM] * 3 + [HBM] * 6,
        [pltpu.VMEM((COUNTS[3], strides[DEGREE], lanes), F32), pltpu.VMEM((2, *pieces[0].shape), F32)]
        + [pltpu.VMEM((3, *fields.shape), F32), pltpu.SemaphoreType.DMA((6,))]
        + [pltpu.VMEM((DIMS, strides[DEGREE], lanes), F32), pltpu.VMEM((2, DIMS, 3 * widths[DEGREE], lanes), F32)]
        + [pltpu.VMEM((COUNTS[DEGREE], strides[DEGREE], lanes), F32), pltpu.VMEM((2, COUNTS[DEGREE], 3 * widths[DEGREE], lanes), F32)]
        + [pltpu.VMEM((9 * height2, 27 * height), BF16), table, pltpu.VMEM((2 * UNROLL, 4, 3 * height, lanes), F32)]
        + splits(2 * UNROLL, 4, 3 * height),
        [slot_term, weights, taps, image, even, odd, fields, *fields_pair],
        "level_last",
        COUNTS[DEGREE] * 2 * 27 * 9 * height * height2 * 256,
        63,
    )
    result, middle = lax.optimization_barrier((result, middle))
    final = exchange(result.reshape(groups, -1, lanes))
    partial = call(
        functools.partial(assemble_kernel, own, starts[DEGREE]),
        pltpu.HBM(forcing.shape, F32),
        [SMEM] + [VMEM] * (DEGREE + 1),
        [],
        [slot_term, part01, part2, part3, part4, middle],
        "assemble",
        0,
        60,
    )
    partial, final = lax.optimization_barrier((partial, final))
    return pl.pallas_call(
        functools.partial(finish_kernel, own, starts[DEGREE]),
        out_shape=array(*forcing.shape),
        in_specs=[SMEM, ANY, ANY],
        out_specs=ANY,
        scratch_shapes=[pltpu.VMEM((caps[DEGREE], *field), F32), pltpu.VMEM(final.shape, F32), pltpu.SemaphoreType.DMA((1 + caps[DEGREE],))],
        input_output_aliases={1: 0},
        compiler_params=pltpu.CompilerParams(vmem_limit_bytes=60 * 2**20),
        name="finish",
    )(slot_term, partial, final)


def solution(mesh):
    return jax.shard_map(
        on_device,
        mesh=mesh,
        in_specs=(
            P("terms", None, "space", None, None),
            P(),
            P(None, "space", None, None),
            P(),
            P(),
        ),
        out_specs=P("terms", None, "space", None, None),
        check_vma=False,
    )
```

```python
import functools
import math

import jax
import jax.numpy as jnp
import numpy as np
from jax import lax
from jax.experimental import pallas as pl
from jax.experimental.pallas import tpu as pltpu
from jax.sharding import PartitionSpec as P

DIMS = 5
DEGREE = 4
UNROLL = {1: 5, 2: 15, 3: 35, 4: 35}
F32 = jnp.float32
BF16 = jnp.bfloat16
ANY = pl.BlockSpec(memory_space=pl.ANY)
VMEM = pl.BlockSpec(memory_space=pltpu.VMEM)
HBM = pl.BlockSpec(memory_space=pltpu.HBM)
SMEM = pl.BlockSpec(memory_space=pltpu.SMEM)


def compositions(total, pieces_left):
    if pieces_left == 1:
        return [[total]]
    result = []
    for leading in range(total, -1, -1):
        for remainder in compositions(total - leading, pieces_left - 1):
            result.append([leading] + remainder)
    return result


def chaos_links():
    indices = []
    for level in range(DEGREE + 1):
        indices.extend(compositions(level, DIMS))
    lookup = {tuple(vector): number for number, vector in enumerate(indices)}
    dims = np.zeros((len(indices), DEGREE), np.int32)
    parents = np.full((len(indices), DEGREE), -1, np.int32)
    for number, vector in enumerate(indices):
        place = 0
        for dim in range(DIMS):
            if vector[dim] > 0:
                lowered = list(vector)
                lowered[dim] -= 1
                dims[number, place] = dim
                parents[number, place] = lookup[tuple(lowered)]
                place += 1
    return dims, parents


LINK_DIMS, LINK_PARENTS = chaos_links()
COUNTS = [math.comb(level + DIMS - 1, DIMS - 1) for level in range(DEGREE + 1)]
FIRSTS = [sum(COUNTS[:level]) for level in range(DEGREE + 1)]


def matrix_kernel(stencil_ref, packed_ref):
    fill_matrix(0, stencil_ref, packed_ref)


def fill_matrix(shift, stencil_ref, packed_ref):
    size = packed_ref.shape[1] // 3
    rows = size // 9
    out_rows = packed_ref.shape[0] // 9
    lane = lax.broadcasted_iota(jnp.int32, (out_rows, size), 1)
    step = lane % rows - lax.broadcasted_iota(jnp.int32, (out_rows, size), 0) + (1 - shift)
    column = lane // rows
    for oz in range(3):
        for a in range(3):
            block = jnp.zeros((out_rows, size), F32)
            for oy in range(3):
                taps = jnp.zeros((out_rows, size), F32)
                for ox in range(3):
                    for b in range(3):
                        taps = jnp.where(column == 3 * ox + b, stencil_ref[a, b, 9 * ox + 3 * oy + oz], taps)
                block = jnp.where(step == oy, taps, block)
            high = block.astype(BF16)
            place = pl.ds((3 * oz + a) * out_rows, out_rows)
            packed_ref[place, :size] = high
            packed_ref[place, size : 2 * size] = high
            packed_ref[place, 2 * size :] = (block - high.astype(F32)).astype(BF16)


def put_split(value, high_ref, low_ref, place):
    high = value.astype(BF16)
    high_ref[place] = high
    low_ref[place] = (value - high.astype(F32)).astype(BF16)


def apply_pair(high_ref, low_ref, packed_ref, place):
    def window(ref):
        return [jnp.concatenate([ref[place + k], ref[place + k + 1]], axis=1) for k in range(3)]

    high = window(high_ref)
    operand = jnp.concatenate(high + window(low_ref) + high, axis=0)
    product = jnp.dot(packed_ref[...], operand, preferred_element_type=F32)
    lanes = high_ref.shape[2]
    size = packed_ref.shape[0] // 3
    lane = lax.broadcasted_iota(jnp.int32, (size, lanes), 1)
    results = []
    for half in range(2):
        block = product[:, half * lanes : (half + 1) * lanes]
        before = pltpu.roll(block[:size], 1, 1)
        after = pltpu.roll(block[2 * size :], lanes - 1, 1)
        results.append(block[size : 2 * size] + jnp.where(lane > 0, before, 0.0) + jnp.where(lane < lanes - 1, after, 0.0))
    return results


def start_copies(sources, targets, semaphores):
    copies = [pltpu.make_async_copy(source, target, semaphores.at[i]) for i, (source, target) in enumerate(zip(sources, targets, strict=True))]
    for copy in copies:
        copy.start()
    return copies


def eight(rows):
    return (rows + 7) // 8 * 8


def inverse_pivots(stencil_ref, rows, lanes):
    return jnp.concatenate([1.0 / jnp.full((rows, lanes), stencil_ref[a, a, 13], F32) for a in range(3)], axis=0)


def edge_flags():
    slab = lax.axis_index("space")
    return slab % 2 == 0, slab > 0, slab < lax.axis_size("space") - 1


def window(start, width, rows):
    first = max(start, 0)
    last = min(start + width, rows)
    return first, first - start, last - first


def fields_window(own, halo, layers, fields_ref, out):
    group = lax.axis_index("terms")
    rows, lanes = fields_ref.shape[2:]
    width = own + 2 * halo
    for case in range(lax.axis_size("terms")):

        @pl.when(group == case)
        def _():
            first, place, length = window(own * case - halo, width, rows)
            for dim in range(DIMS):
                for plane in range(3 * len(layers)):
                    base = plane * width
                    if place:
                        out[dim, base : base + place] = jnp.zeros((place, lanes), F32)
                    out[dim, base + place : base + place + length] = fields_ref[dim, layers[plane % len(layers)], first : first + length]
                    if place + length < width:
                        out[dim, base + place + length : base + width] = jnp.zeros((width - place - length, lanes), F32)


def link_sums(level, coupling_ref, modes, image_of, out):
    for child in range(COUNTS[level]):
        number = FIRSTS[level] + child
        total = 0.0
        for dim, parent in zip(LINK_DIMS[number], LINK_PARENTS[number], strict=True):
            if parent >= 0:
                total = total - (modes[int(dim)] * coupling_ref[int(dim), number]) * image_of(int(parent) - FIRSTS[level - 1])
        out[child] = total


def places(place, start, cap, stride, offset, groups, slot_dev, slot_ref):
    for source in range(groups):
        for slot in range(cap):
            term = slot_ref[source * slot_dev + start + slot]
            place[jnp.where(term >= 0, term, 127)] = source * stride + offset + slot


def own_kernel(own, first, layout, stencil_ref, packed, forcing_ref, even_ref, odd_ref, settled_ref, out_ref, image, high, low, high2, low2):
    rows, lanes = forcing_ref.shape[3:]
    size = 3 * rows
    groups = out_ref.shape[0]
    inverse = inverse_pivots(stencil_ref, rows, lanes)
    is_even, has_lower, has_upper = edge_flags()

    def load(number, x):
        slot = first + number
        if 2 <= x < 4:
            return forcing_ref[slot, :, x - 2].reshape(size, lanes)
        even = even_ref[slot, :, x % 2].reshape(size, lanes)
        odd = odd_ref[slot, :, x % 2].reshape(size, lanes)
        return jnp.where(is_even, odd, even) if x < 2 else jnp.where(is_even, even, odd)

    for number in range(len(layout)):
        for x in range(6):
            put_split(load(number, x) * inverse, high.at[number], low.at[number], x)
    for number in range(len(layout)):
        for pair in range(2):
            applied = apply_pair(high.at[number], low.at[number], packed, 2 * pair)
            for half in range(2):
                x = 2 * pair + half + 1
                load_x = load(number, x)
                value = load_x * inverse + (load_x - applied[half]) * inverse
                if x == 1:
                    value = jnp.where(has_lower, value, 0.0)
                if x == 4:
                    value = jnp.where(has_upper, value, 0.0)
                if 2 <= x < 4:
                    settled_ref[number, :, x - 2] = value.reshape(3, rows, lanes)
                put_split(value, high2.at[number], low2.at[number], x - 1)
    for number, (halo, row) in enumerate(layout):
        applied = apply_pair(high2.at[number], low2.at[number], packed, 0)
        for x in range(2):
            image[number, x] = applied[x]
        width = own + 2 * halo
        for group in range(groups):
            begin, place, length = window(own * group - halo, width, rows)
            for plane in range(6):
                target = row + plane * width
                start = plane // 2 * rows + begin
                if place:
                    out_ref[group, target : target + place] = jnp.zeros((place, lanes), F32)
                out_ref[group, target + place : target + place + length] = image[number, plane % 2, start : start + length]
                if place + length < width:
                    out_ref[group, target + place + length : target + width] = jnp.zeros((width - place - length, lanes), F32)


def own_last_kernel(first, stencil_ref, packed, forcing_ref, even_ref, odd_ref, settled_ref, high, low):
    rows, lanes = forcing_ref.shape[3:]
    size = 3 * rows
    inverse = inverse_pivots(stencil_ref, rows, lanes)
    is_even = edge_flags()[0]
    for number in range(settled_ref.shape[0]):
        even = even_ref[number].reshape(size, lanes)
        odd = odd_ref[number].reshape(size, lanes)
        put_split(jnp.where(is_even, odd, even) * inverse, high.at[number], low.at[number], 0)
        put_split(jnp.where(is_even, even, odd) * inverse, high.at[number], low.at[number], 3)
        for x in range(2):
            put_split(forcing_ref[first + number, :, x].reshape(size, lanes) * inverse, high.at[number], low.at[number], x + 1)
        applied = apply_pair(high.at[number], low.at[number], packed, 0)
        for x in range(2):
            load = forcing_ref[first + number, :, x].reshape(size, lanes)
            value = load * inverse + (load - applied[x]) * inverse
            settled_ref[number, :, x] = value.reshape(3, rows, lanes)


def first_kernel(groups, slot_dev, slot_ref, image_ref, out_ref):
    source = jnp.int32(0)
    for group in range(groups):
        source = jnp.where(slot_ref[group * slot_dev] >= 0, group, source)
    out_ref[0] = image_ref[source, : out_ref.shape[1]]


def level_kernel(level, own, halo, rows, caps, starts, base, slot_dev, slot_ref, coupling_ref, stencil_ref, own_hbm, even_hbm, odd_hbm, fields_hbm, fields_even, fields_odd, image_ref, *refs):
    slabs, fields, semaphores, modes, loads, packed, packed2, in_place, out_place, ext, ext2, high, low, high2, low2 = refs[-15:]
    olds = refs[:1] if level > 1 else ()
    is_even, has_lower, has_upper = edge_flags()
    side = jnp.where(is_even, 2, 0)
    places_of = (1, side, 2 - side)
    copies = start_copies(
        (own_hbm, even_hbm, odd_hbm, fields_hbm, fields_even, fields_odd),
        [slabs.at[place] for place in places_of] + [fields.at[place] for place in places_of],
        semaphores,
    )
    settled_ref, images, *pieces = refs[len(olds) : -15]
    unroll = UNROLL[level]
    groups = lax.axis_size("terms")
    group = lax.axis_index("terms")
    lanes = images.shape[2]
    width = own + 2 * halo
    height, height2, height3 = eight(width), eight(width - 2), eight(width - 4)
    next_width = width - 4
    offset = sum(caps[1:level])
    stride = offset + caps[level]
    places(in_place, starts[level], caps[level], caps[level], 0, groups, slot_dev, slot_ref)
    places(out_place, starts[level], caps[level], stride, offset, groups, slot_dev, slot_ref)
    inverse = inverse_pivots(stencil_ref, height, lanes)
    inverse2 = inverse_pivots(stencil_ref, height2, lanes)
    place = lax.broadcasted_iota(jnp.int32, (3 * height2, lanes), 0) % height2 + (own * group - halo + 1)
    inside = ((place >= 0) & (place < rows)).astype(F32)
    ext[...] = jnp.zeros(ext.shape, F32)
    ext2[...] = jnp.zeros(ext2.shape, F32)
    fill_matrix(1, stencil_ref, packed)
    fill_matrix(1, stencil_ref, packed2)
    for copy in copies:
        copy.wait()
    for slab in range(3):
        fields_window(own, halo, (0, 1), fields.at[slab], modes.at[slab])
        link_sums(level, coupling_ref, modes.at[slab], lambda parent, slab=slab: slabs[slab, parent], loads.at[slab])
    for old_ref in olds:
        for source in range(groups):
            settled_ref[source * stride : source * stride + offset] = old_ref[source * offset : (source + 1) * offset]

    def terms(step, carry):
        lanes_of = [(lane, step * unroll + lane) for lane in range(unroll)]
        for lane, term in lanes_of:
            for x in range(6):
                for a in range(3):
                    start = (2 * a + x % 2) * width
                    value = loads[x // 2, term, start : start + width]
                    ext[lane, x, a * height : a * height + width] = value
                    if 1 <= x < 5:
                        ext2[lane, x - 1, a * height2 : a * height2 + width - 2] = value[1 : width - 1]
                put_split(ext[lane, x] * inverse, high.at[lane], low.at[lane], x)
        for lane, term in lanes_of:
            out_slot = out_place[FIRSTS[level] + term]
            for pair in range(2):
                applied = apply_pair(high.at[lane], low.at[lane], packed, 2 * pair)
                for half in range(2):
                    x = 2 * pair + half
                    load = ext2[lane, x]
                    value = (load * inverse2 + (load - applied[half]) * inverse2) * inside
                    if x == 0:
                        value = jnp.where(has_lower, value, 0.0)
                    if x == 3:
                        value = jnp.where(has_upper, value, 0.0)
                    if 1 <= x < 3:
                        for a in range(3):
                            plane = 2 * a + x - 1
                            begin = a * height2 + halo - 1
                            settled_ref[out_slot, plane * own : (plane + 1) * own] = value[begin : begin + own]
                    put_split(value, high2.at[lane], low2.at[lane], x)
        for lane, term in lanes_of:
            in_slot = in_place[FIRSTS[level] + term]
            applied = apply_pair(high2.at[lane], low2.at[lane], packed2, 0)
            for a in range(3):
                for x in range(2):
                    begin = (2 * a + x) * next_width
                    part = pl.ds(begin, next_width)
                    images[term, part] = applied[x][a * height3 : a * height3 + next_width] + image_ref[in_slot, pl.ds(base + begin, next_width)]
        return carry

    lax.fori_loop(0, COUNTS[level] // unroll, terms, 0)

    if pieces:
        for term in range(COUNTS[level]):
            for a in range(3):
                layers = [images[term, (2 * a + x) * next_width : (2 * a + x + 1) * next_width] for x in range(2)]
                begin = (3 * (term % 4) + a) * next_width
                pieces[0][term // 4, begin : begin + next_width] = jnp.where(is_even, layers[1], layers[0])
                pieces[1][term // 4, begin : begin + next_width] = jnp.where(is_even, layers[0], layers[1])


def last_kernel(own, caps, starts, slot_dev, slot_ref, coupling_ref, stencil_ref, own_hbm, even_hbm, odd_hbm, fields_hbm, fields_even, fields_odd, settled_ref, images, sides, fields, semaphores, modes, side_modes, loads, side_loads, packed, place, ext, high, low):
    groups = lax.axis_size("terms")
    lanes = settled_ref.shape[2]
    width = own + 2
    height, height2 = eight(width), eight(own)
    side = jnp.where(edge_flags()[0], 1, 0)
    copies = start_copies(
        (own_hbm, even_hbm, odd_hbm, fields_hbm, fields_even, fields_odd),
        (images, sides.at[side], sides.at[1 - side], fields.at[2], fields.at[side], fields.at[1 - side]),
        semaphores,
    )
    places(place, starts[DEGREE], caps[DEGREE], caps[DEGREE], 0, groups, slot_dev, slot_ref)
    inverse = inverse_pivots(stencil_ref, height, lanes)
    ext[...] = jnp.zeros(ext.shape, F32)
    fill_matrix(1, stencil_ref, packed)
    for copy in copies:
        copy.wait()
    fields_window(own, 1, (0, 1), fields.at[2], modes)
    link_sums(DEGREE, coupling_ref, modes, lambda parent: images[parent], loads)
    for upper in range(2):

        def side_image(parent, upper=upper):
            begin = 3 * (parent % 4) * width
            return sides[upper, parent // 4, begin : begin + 3 * width]

        fields_window(own, 1, (1 - upper,), fields.at[upper], side_modes.at[upper])
        link_sums(DEGREE, coupling_ref, side_modes.at[upper], side_image, side_loads.at[upper])

    def terms(step, carry):
        for lane in range(UNROLL[DEGREE]):
            term = step * UNROLL[DEGREE] + lane
            for a in range(3):
                for upper in range(2):
                    ext[lane, 3 * upper, a * height : a * height + width] = side_loads[upper, term, a * width : (a + 1) * width]
                for x in range(2):
                    begin = (2 * a + x) * width
                    ext[lane, x + 1, a * height : a * height + width] = loads[term, begin : begin + width]
            for x in range(4):
                put_split(ext[lane, x] * inverse, high.at[lane], low.at[lane], x)
        for lane in range(UNROLL[DEGREE]):
            term = step * UNROLL[DEGREE] + lane
            applied = apply_pair(high.at[lane], low.at[lane], packed, 0)
            slot = place[FIRSTS[DEGREE] + term]
            for a in range(3):
                scale = inverse[a * height : a * height + own]
                for x in range(2):
                    begin = (2 * a + x) * width + 1
                    load = loads[term, begin : begin + own]
                    plane = 2 * a + x
                    settled_ref[slot, plane * own : (plane + 1) * own] = load * scale + (load - applied[x][a * height2 : a * height2 + own]) * scale
        return carry

    lax.fori_loop(0, COUNTS[DEGREE] // UNROLL[DEGREE], terms, 0)


def assemble_kernel(own, start, slot_ref, *refs):
    *parts, links_ref, out_ref = refs
    slot_dev, _, _, rows, lanes = out_ref.shape
    groups = rows // own
    first = lax.axis_index("terms") * slot_dev
    out_ref[0] = jnp.where(slot_ref[first] >= 0, parts[0][0], 0.0)
    begin = 1
    for number, part in enumerate(parts):
        skip = 1 if number == 0 else 0
        for slot in range(part.shape[0] - skip):
            filled = slot_ref[first + begin] >= 0
            for plane in range(6):
                place = ((begin - 1) * 6 + plane) * own
                value = part[skip + slot, plane // 2, plane % 2]
                if begin < start:
                    value = value + jnp.concatenate([links_ref[group, place : place + own] for group in range(groups)], axis=0)
                out_ref[begin, plane // 2, plane % 2] = jnp.where(filled, value, 0.0)
            begin += 1


def finish_kernel(own, start, slot_ref, partial_ref, links_hbm, out_ref, block, links_ref, semaphores):
    slot_dev = out_ref.shape[0]
    rows = out_ref.shape[3]
    count = slot_dev - start
    groups = rows // own
    first = lax.axis_index("terms") * slot_dev + start
    copies = start_copies([links_hbm, *[partial_ref.at[start + slot] for slot in range(count)]], [links_ref, *[block.at[slot] for slot in range(count)]], semaphores)
    copies.pop(0).wait()
    back = [pltpu.make_async_copy(block.at[slot], out_ref.at[start + slot], semaphores.at[1 + slot]) for slot in range(count)]
    for slot in range(count):
        copies[slot].wait()
        filled = slot_ref[first + slot] >= 0
        for plane in range(6):
            place = (slot * 6 + plane) * own
            value = jnp.concatenate([links_ref[group, place : place + own] for group in range(groups)], axis=0)
            block[slot, plane // 2, plane % 2] += jnp.where(filled, value, 0.0)
        back[slot].start()
    for copy in back:
        copy.wait()


def call(kernel, out_shape, specs, scratch, operands, name, flops=0, megabytes=12):
    single = not isinstance(out_shape, list)
    return pl.pallas_call(
        kernel,
        out_shape=out_shape,
        in_specs=specs,
        out_specs=VMEM if single else [VMEM] * len(out_shape),
        scratch_shapes=scratch,
        compiler_params=pltpu.CompilerParams(vmem_limit_bytes=megabytes * 2**20),
        cost_estimate=pl.CostEstimate(flops=flops, bytes_accessed=sum(4 * math.prod(o.shape) for o in operands), transcendentals=0),
        name=name,
    )(*operands)


def beside(array, axis):
    count = lax.axis_size(axis)
    even = [(i, i ^ 1) for i in range(count)]
    odd = [(i, ((i + 1) ^ 1) - 1) for i in range(1, count - 1)]
    return lax.ppermute(array[0], axis, even), lax.ppermute(array[1], axis, odd)


def exchange(blocks):
    return lax.all_to_all(blocks, "terms", 0, 0, tiled=True)


def on_device(forcing, stencil, fields, coupling, slot_term):
    groups = lax.axis_size("terms")
    slot_dev = forcing.shape[0]
    caps = [(count + groups - 1) // groups for count in COUNTS]
    starts = [sum(caps[:level]) for level in range(DEGREE + 1)]
    rows, lanes = forcing.shape[3:]
    field = forcing.shape[1:]
    own = rows // groups
    halos = [None] + [2 * (DEGREE - level) + 1 for level in range(1, DEGREE + 1)]
    widths = [None] + [own + 2 * halo for halo in halos[1:]]
    strides = [None] + [eight(6 * width) for width in widths[1:]]

    def array(*shape):
        return jax.ShapeDtypeStruct(shape, F32)

    taps = jnp.transpose(stencil, (1, 2, 0))
    weights = coupling.T
    whole = call(matrix_kernel, jax.ShapeDtypeStruct((9 * rows, 27 * rows), BF16), [SMEM], [], [taps], "matrix")

    def splits(lead, layers, size):
        return [pltpu.VMEM((lead, layers, size, lanes), BF16)] * 2

    def own_part(slots, beside_pair, base, levels):
        layout, row = [], 0
        for level in levels:
            for _ in range(caps[level]):
                layout.append((halos[level + 1], row))
                row += strides[level + 1] if len(levels) == 1 else 6 * widths[level + 1]
        row = eight(row)
        count = len(layout)
        size = 3 * rows
        return call(
            functools.partial(own_kernel, own, starts[levels[0]] - base, layout),
            [pltpu.HBM((count, *field), F32), pltpu.HBM((groups, row, lanes), F32)],
            [SMEM] + [VMEM] * 4,
            [pltpu.VMEM((count, 2, size, lanes), F32)] + splits(count, 6, size) + splits(count, 4, size),
            [taps, whole, slots, *beside_pair],
            "own",
            count * 3 * 2 * 27 * size * size * 256,
        )

    front = forcing[: starts[2]]
    part01, packed = own_part(front, beside((front, front), "space"), 0, (0, 1))
    packed, forcing, fields = lax.optimization_barrier((packed, forcing, fields))
    back2, back3 = forcing[starts[2] : starts[3]], forcing[starts[3] : starts[4]]
    part2, packed2 = own_part(back2, beside((back2, back2), "space"), starts[2], (2,))
    part3, packed3 = own_part(back3, beside((back3, back3), "space"), starts[3], (3,))
    fields_pair = beside((fields, fields), "space")
    is_even = lax.axis_index("space") % 2 == 0
    layers = [forcing[starts[4] :, :, x] for x in range(2)]
    borders = (jnp.where(is_even, layers[1], layers[0]), jnp.where(is_even, layers[0], layers[1]))
    front_images, packed2, fields_pair = lax.optimization_barrier((exchange(packed), packed2, fields_pair))
    def own_last(pair):
        return call(
            functools.partial(own_last_kernel, starts[4]),
            pltpu.HBM((caps[4], *field), F32),
            [SMEM] + [VMEM] * 4,
            splits(caps[4], 4, 3 * rows),
            [taps, whole, forcing, *pair],
            "own_last",
            caps[4] * 2 * 27 * 9 * rows * rows * 256,
        )

    image = call(
        functools.partial(first_kernel, groups, slot_dev),
        pltpu.HBM((1, strides[1], lanes), F32),
        [SMEM, VMEM],
        [],
        [slot_term, front_images],
        "first",
    )
    arrived = [None, front_images, exchange(packed2), None]
    table = pltpu.SMEM((128,), jnp.int32)
    settled = []
    for level in range(1, DEGREE):
        height, height2 = eight(widths[level]), eight(widths[level] - 2)
        base = 6 * widths[1] if level == 1 else 0
        part = arrived[level].reshape(groups * (1 if level == 1 else caps[level]), -1, lanes)
        olds = settled
        total = sum(caps[1 : level + 1])
        shapes = [pltpu.HBM((groups * total, 6 * own, lanes), F32), pltpu.HBM((COUNTS[level], strides[level + 1], lanes), F32)]
        if level == DEGREE - 1:
            shapes += [pltpu.HBM(((COUNTS[level] + 3) // 4, 12 * widths[DEGREE], lanes), F32)] * 2
        size, size2 = 3 * height, 3 * height2
        even, odd = beside((image, image), "space")
        if level == 1:
            even, packed3 = lax.optimization_barrier((even, packed3))
        if level == 2:
            even, packed3 = lax.optimization_barrier((even, packed3))
            arrived[3] = exchange(packed3)
        result, image, *pieces = call(
            functools.partial(level_kernel, level, own, halos[level], rows, caps, starts, base, slot_dev),
            shapes,
            [SMEM] * 3 + [HBM] * 6 + [VMEM] * (1 + len(olds)),
            [pltpu.VMEM((3, COUNTS[level - 1], strides[level], lanes), F32), pltpu.VMEM((3, *fields.shape), F32), pltpu.SemaphoreType.DMA((6,))]
            + [pltpu.VMEM((3, DIMS, strides[level], lanes), F32), pltpu.VMEM((3, COUNTS[level], strides[level], lanes), F32)]
            + [pltpu.VMEM((3 * size2, 9 * size), BF16), pltpu.VMEM((9 * eight(widths[level] - 4), 9 * size2), BF16)]
            + [table, table]
            + [pltpu.VMEM((UNROLL[level], 6, size, lanes), F32), pltpu.VMEM((UNROLL[level], 4, size2, lanes), F32)]
            + splits(UNROLL[level], 6, size)
            + splits(UNROLL[level], 4, size2),
            [slot_term, weights, taps, image, even, odd, fields, *fields_pair, part, *olds],
            "level",
            (1 if level == 1 else 30) * COUNTS[level] * 2 * 27 * size2 * (2 * size + size2) * 256,
            63,
        )
        settled = [result]
    middle = exchange(result.reshape(groups, -1, lanes))
    even, odd = beside(pieces, "space")
    even, odd, borders = lax.optimization_barrier((even, odd, borders))
    part4 = own_last(beside(borders, "space"))
    height, height2 = eight(widths[DEGREE]), eight(own)
    result = call(
        functools.partial(last_kernel, own, caps, starts, slot_dev),
        pltpu.HBM((groups * caps[DEGREE], 6 * own, lanes), F32),
        [SMEM] * 3 + [HBM] * 6,
        [pltpu.VMEM((COUNTS[3], strides[DEGREE], lanes), F32), pltpu.VMEM((2, *pieces[0].shape), F32)]
        + [pltpu.VMEM((3, *fields.shape), F32), pltpu.SemaphoreType.DMA((6,))]
        + [pltpu.VMEM((DIMS, strides[DEGREE], lanes), F32), pltpu.VMEM((2, DIMS, 3 * widths[DEGREE], lanes), F32)]
        + [pltpu.VMEM((COUNTS[DEGREE], strides[DEGREE], lanes), F32), pltpu.VMEM((2, COUNTS[DEGREE], 3 * widths[DEGREE], lanes), F32)]
        + [pltpu.VMEM((9 * height2, 27 * height), BF16), table, pltpu.VMEM((UNROLL[DEGREE], 4, 3 * height, lanes), F32)]
        + splits(UNROLL[DEGREE], 4, 3 * height),
        [slot_term, weights, taps, image, even, odd, fields, *fields_pair],
        "level_last",
        COUNTS[DEGREE] * 2 * 27 * 9 * height * height2 * 256,
        63,
    )
    result, middle = lax.optimization_barrier((result, middle))
    final = exchange(result.reshape(groups, -1, lanes))
    partial = call(
        functools.partial(assemble_kernel, own, starts[DEGREE]),
        pltpu.HBM(forcing.shape, F32),
        [SMEM] + [VMEM] * (DEGREE + 1),
        [],
        [slot_term, part01, part2, part3, part4, middle],
        "assemble",
        0,
        60,
    )
    partial, final = lax.optimization_barrier((partial, final))
    return pl.pallas_call(
        functools.partial(finish_kernel, own, starts[DEGREE]),
        out_shape=array(*forcing.shape),
        in_specs=[SMEM, ANY, ANY],
        out_specs=ANY,
        scratch_shapes=[pltpu.VMEM((caps[DEGREE], *field), F32), pltpu.VMEM(final.shape, F32), pltpu.SemaphoreType.DMA((1 + caps[DEGREE],))],
        input_output_aliases={1: 0},
        compiler_params=pltpu.CompilerParams(vmem_limit_bytes=60 * 2**20),
        name="finish",
    )(slot_term, partial, final)


def solution(mesh):
    return jax.shard_map(
        on_device,
        mesh=mesh,
        in_specs=(
            P("terms", None, "space", None, None),
            P(),
            P(None, "space", None, None),
            P(),
            P(),
        ),
        out_specs=P("terms", None, "space", None, None),
        check_vma=False,
    )
```
